128 devices in a mesh: dp: 16 (over z, x_hi, core), pipe: 8 (over x_lo, y).
Axes of the slice: x: 4 (x_hi: 2, x_lo: 2; x = x_hi * 2 + x_lo), y: 4, z: 4, core: 2. Of those that a mesh axis runs over, the one named last changes fastest.
Arguments:
- inputs: bfloat16 [4, 1024, 8192], P(None, 'dp'), may hold values from -6 to 6
- targets: int32 [4, 1024], P(None, 'dp'), may hold values from 0 to 511
- adapter_down: bfloat16 [8, 8192, 256], P('pipe'), may hold values from -0.0625 to 0.0625
- adapter_up: bfloat16 [8, 256, 8192], P('pipe'), may hold values from -0.375 to 0.375
- value_weight: float32 [8192], replicated, may hold values from -0.0625 to 0.0625
- returns: float32 [512], replicated, may hold values from -6 to 6
Outputs:
- grad_down: float32 [8, 8192, 256], P('pipe', 'dp')
- grad_up: float32 [8, 256, 8192], P('pipe', None, 'dp')
The draws below stay inside these ranges and needn't reach their ends.
All inputs are finite; a program needn't handle non-finite values.
Results may differ from the reference program's by a relative error of at most 0.024.
Values may be sent and summed in bfloat16 or wider, within the bound.
A program may use at most 128 MiB of HBM per device.

```python
import jax
import jax.numpy as jnp
from jax import lax

D = 8192
R = 256
MICRO = 4
AGENTS = 512
LAYERS = 8
ROWS = 1024


def place_ends(entries, key, least, high):
    longest = entries.shape.index(max(entries.shape))
    spots = []
    for shift in (0, 1):
        where = [jax.random.randint(jax.random.fold_in(key, axis), (), 0, length) for axis, length in enumerate(entries.shape)]
        where[longest] = (where[longest] + shift) % entries.shape[longest]
        spots.append(tuple(where))
    return entries.at[spots[0]].set(least).at[spots[1]].set(high)


def strengthened(result, rng, source, target, blocks, factor):
    owner, partner = [(jnp.arange(result.shape[dim]) // (result.shape[dim] // blocks)).reshape([-1 if axis == dim else 1 for axis in range(result.ndim)]) for dim in (source, target)]
    chosen = jax.random.permutation(rng, blocks)[partner]
    strong = (owner == chosen) | (owner == (partner + blocks // 2) % blocks)
    return jnp.where(strong, factor * result, result)


def level_of(key, shape, shards, low, largest):
    factor_of = 1.0
    for position, shards_of in shards:
        heights = jax.random.uniform(jax.random.fold_in(jax.random.fold_in(key, 6), position), (shards_of,), jnp.float32, low / len(shards), largest / len(shards))
        factor_of = factor_of * jnp.repeat(jnp.exp(heights), shape[position] // shards_of).reshape((-1,) + (1,) * (len(shape) - 1 - position))
    return factor_of


def centred(own_key, extent, spread, reach, shards=(), dtype=jnp.bfloat16):
    level = level_of(own_key, extent, shards, -0.22, 0.18) if shards else 1.0
    array = jax.random.normal(own_key, extent, jnp.float32) * spread * level
    return jnp.minimum(jnp.maximum(array, -reach), reach).astype(dtype)


def heavy_noise(rng, shape, deviation, limit, shards, heavy, kind=jnp.bfloat16):
    drawn = deviation * jax.random.normal(rng, shape, jnp.float32)
    if shards:
        drawn = drawn * level_of(rng, shape, shards, -0.22, 0.18)
    return jnp.clip(strengthened(drawn, jax.random.fold_in(rng, 3), *heavy), -limit, limit).astype(kind)


def setup_inputs(seed: int = 0) -> dict:
    streams_of = jax.random.split(jax.random.key(seed), 7)
    return {
        "inputs": heavy_noise(streams_of[0], (MICRO, ROWS, D), 1.0, 6.0, ((1, 16),), (1, 2, 16, 2.0)),
        "targets": place_ends(jax.random.randint(streams_of[1], (MICRO, ROWS), 0, AGENTS), jax.random.fold_in(streams_of[1], 1), 0, AGENTS - 1).astype(jnp.int32),
        "adapter_down": centred(streams_of[2], (LAYERS, D, R), D ** -0.5, 0.0625, ((0, 8),)),
        "adapter_up": centred(streams_of[3], (LAYERS, R, D), R ** -0.5, 0.375, ((0, 8),)),
        "value_weight": centred(streams_of[4], (D,), D ** -0.5, 0.0625, (), jnp.float32),
        "returns": centred(streams_of[5], (AGENTS,), 1.0, 6.0, (), jnp.float32),
    }


def norm_rows(values):
    floats = values.astype(jnp.float32)
    factor = lax.rsqrt(lax.optimization_barrier(jnp.mean(floats * floats, axis=-1, keepdims=True)) + 1e-05)
    return (floats * factor, factor)

def layer_forward(layer_in, w_down, w_up):
    normed_f, factor = norm_rows(layer_in)
    pre = jnp.dot(normed_f.astype(jnp.bfloat16), w_down, preferred_element_type=jnp.float32)
    act = jax.nn.silu(pre).astype(jnp.bfloat16)
    out = (layer_in.astype(jnp.float32) + jnp.dot(act, w_up, preferred_element_type=jnp.float32)).astype(jnp.bfloat16)
    return (out, pre, act)

def layer_backward(layer_in, pre, grad_out, w_down, w_up):
    normed_f, factor = norm_rows(layer_in)
    grad_act = jnp.dot(grad_out, w_up.T, preferred_element_type=jnp.float32)
    sigma = jax.nn.sigmoid(pre)
    grad_pre = (grad_act * sigma * (1.0 + pre * (1.0 - sigma))).astype(jnp.bfloat16)
    grad_norm = jnp.dot(grad_pre, w_down.T, preferred_element_type=jnp.float32)
    inner = lax.optimization_barrier(jnp.mean(grad_norm * normed_f, axis=-1, keepdims=True))
    grad_in = (grad_out.astype(jnp.float32) + factor * (grad_norm - normed_f * inner)).astype(jnp.bfloat16)
    return (grad_in, normed_f.astype(jnp.bfloat16), grad_pre)

def value_grad(final, target_values, value_weight):
    normed_f, factor = norm_rows(final)
    value = lax.optimization_barrier(jnp.sum(normed_f * value_weight, axis=-1))
    resid = value - target_values
    pulled = resid[..., None] * value_weight
    inner = lax.optimization_barrier(jnp.mean(pulled * normed_f, axis=-1, keepdims=True))
    return (factor * (pulled - normed_f * inner)).astype(jnp.bfloat16)

def reference(inputs, targets, adapter_down, adapter_up, value_weight, returns):
    layer_count = adapter_down.shape[0]
    target_values = returns[targets]
    grads_down = [jnp.zeros(adapter_down.shape[1:], jnp.float32) for layer in range(layer_count)]
    grads_up = [jnp.zeros(adapter_up.shape[1:], jnp.float32) for layer in range(layer_count)]
    for micro_index in range(MICRO):
        layer_in = inputs[micro_index]
        saved = []
        for layer in range(layer_count):
            out, pre, act = layer_forward(layer_in, adapter_down[layer], adapter_up[layer])
            saved.append((layer_in, pre, act))
            layer_in = out
        grad_out = value_grad(layer_in, target_values[micro_index], value_weight)
        for layer in range(layer_count - 1, -1, -1):
            kept_in, pre, act = saved[layer]
            grad_in, normed, grad_pre = layer_backward(kept_in, pre, grad_out, adapter_down[layer], adapter_up[layer])
            grads_down[layer] = grads_down[layer] + jnp.dot(normed.T, grad_pre, preferred_element_type=jnp.float32)
            grads_up[layer] = grads_up[layer] + jnp.dot(act.T, grad_out, preferred_element_type=jnp.float32)
            grad_out = grad_in
    return (jnp.stack(grads_down), jnp.stack(grads_up))
```

```python
import functools

import jax
import jax.numpy as jnp
from jax import lax
from jax.experimental import pallas as pl
from jax.experimental.pallas import tpu as pltpu
from jax.sharding import PartitionSpec as P

LAYERS = 8
ZN = 4
TOK = 128
OWN = TOK // ZN
CH = 2048
RANK = 256
FEAT = 8192
TILE = 512
F32 = jnp.float32
BF16 = jnp.bfloat16
MESH = pl.DeviceIdType.MESH


def split3(row):
    hi = row.astype(BF16)
    rest = row - hi.astype(F32)
    mid = rest.astype(BF16)
    lo = (rest - mid.astype(F32)).astype(BF16)
    return [hi.astype(F32), mid.astype(F32), lo.astype(F32)]


def pack_rows(rows):
    parts = []
    for row in rows:
        parts += split3(row)
    at = lax.broadcasted_iota(jnp.int32, (16, 128), 0)
    tile = jnp.zeros((16, 128), F32)
    for i, part in enumerate(parts):
        tile = jnp.where(at == i, jnp.broadcast_to(part, (16, 128)), tile)
    return tile.astype(BF16)


def column(row):
    return jnp.transpose(jnp.broadcast_to(row, (TOK, 128)))


def row_sums(acc):
    return jnp.sum(jnp.transpose(acc), axis=0, keepdims=True)


def fold_lanes(tile):
    total = tile[:, 0:128]
    for i in range(1, tile.shape[1] // 128):
        total = total + tile[:, 128 * i : 128 * (i + 1)]
    return total


def wide(col, width):
    return jnp.concatenate([col] * (width // 128), axis=1)


def dot(a, b):
    return lax.dot_general(a, b, (((1,), (0,)), ((), ())), preferred_element_type=F32)


def dot_nt(a, b):
    return lax.dot_general(a, b, (((1,), (1,)), ((), ())), preferred_element_type=F32)


def dot_tn(a, b):
    return lax.dot_general(a, b, (((0,), (0,)), ((), ())), preferred_element_type=F32)


def kernel(
    x_hbm, wd_hbm, wu_hbm, vw_ref, tv_ref, out_hbm,
    xs, wd, wu, snd, rcv, mine, gx, pre_s, act_s, scale_s, gbuf,
    x_ssem, x_rsem, lsem, wsem, ssem, rsem, gsem,
):
    dp = lax.axis_index("dp")
    pipe = lax.axis_index("pipe")
    z = dp // 4
    rest = lax.rem(dp, 4)
    xl = pipe // 4
    y = lax.rem(pipe, 4)
    zs = [lax.rem(z + i, ZN) for i in range(1, ZN)]
    peers = [(zz * 4 + rest, pipe) for zz in zs]

    for layer in range(LAYERS):
        pltpu.make_async_copy(wd_hbm.at[layer], wd.at[layer], wsem.at[0, layer]).start()
        pltpu.make_async_copy(wu_hbm.at[layer], wu.at[layer], wsem.at[1, layer]).start()

    def piece(zz):
        return x_hbm.at[y, pl.ds(pl.multiple_of(xl * OWN, OWN), OWN), pl.ds(pl.multiple_of(zz * CH, CH), CH)]

    own_rows = pl.ds(pl.multiple_of(z * OWN, OWN), OWN)
    own = pltpu.make_async_copy(piece(z), xs.at[0, own_rows], lsem)
    own.start()

    barrier = pltpu.get_barrier_semaphore()
    for peer in peers:
        pl.semaphore_signal(barrier, inc=1, device_id=peer, device_id_type=MESH)
    pl.semaphore_wait(barrier, ZN - 1)

    copies = []
    for i in range(ZN - 1):
        copy = pltpu.make_async_remote_copy(
            src_ref=piece(zs[i]), dst_ref=xs.at[0, own_rows],
            send_sem=x_ssem.at[i], recv_sem=x_rsem.at[i],
            device_id=peers[i], device_id_type=MESH,
        )
        copy.start()
        copies.append(copy)
    own.wait()
    for copy in copies:
        copy.wait()

    def exchange(slot, rows):
        copies = []
        for i in range(ZN - 1):
            copy = pltpu.make_async_remote_copy(
                src_ref=snd.at[slot, pl.ds(0, rows)],
                dst_ref=rcv.at[slot, i, pl.ds(0, rows)],
                send_sem=ssem.at[slot, i], recv_sem=rsem.at[slot, i],
                device_id=peers[i], device_id_type=MESH,
            )
            copy.start()
            copies.append(copy)
        return copies

    def finish(copies):
        for copy in copies:
            copy.wait()

    def wait_weights(which, layer):
        if which == 0:
            pltpu.make_async_copy(wd_hbm.at[layer], wd.at[layer], wsem.at[0, layer]).wait()
        else:
            pltpu.make_async_copy(wu_hbm.at[layer], wu.at[layer], wsem.at[1, layer]).wait()

    def cols(t):
        return slice(t * TILE, (t + 1) * TILE)

    def send_product(slot, product, square):
        mine[...] = product
        snd[slot, 16 : 16 + TOK] = product.astype(BF16)
        row = row_sums(square)
        snd[slot, 0:16, 0:128] = pack_rows([row])
        return row

    def row_total(slot, first, own_row):
        total = own_row
        for i in range(ZN - 1):
            part = rcv[slot, i, 0:16, 0:128].astype(F32)[first : first + 3]
            total = total + jnp.sum(part, axis=0, keepdims=True)
        return total

    snd[...] = jnp.zeros_like(snd)
    wait_weights(0, 0)
    product = jnp.zeros((TOK, RANK), F32)
    square = jnp.zeros((TOK, 128), F32)
    for t in range(CH // TILE):
        tile = xs[0, :, cols(t)]
        wide_tile = tile.astype(F32)
        square += fold_lanes(wide_tile * wide_tile)
        product += dot(tile, wd[0, cols(t), :])
    own_row = send_product(0, product, square)

    def forward(layer, own_row):
        slot = lax.rem(layer, 2)
        copies = exchange(slot, 16 + TOK)
        wait_weights(1, layer)
        finish(copies)
        total = mine[...]
        for i in range(ZN - 1):
            total = total + rcv[slot, i, 16 : 16 + TOK].astype(F32)
        ssq = row_total(slot, 0, own_row)
        scale = column(lax.rsqrt(ssq * (1.0 / FEAT) + 1e-05))
        pre = total * wide(scale, RANK)
        act = (pre / (1.0 + jnp.exp(-pre))).astype(BF16)
        scale_s[layer] = scale
        pre_s[layer] = pre
        act_s[layer] = act
        after = jnp.minimum(layer + 1, LAYERS - 1)

        @pl.when(layer < LAYERS - 1)
        def _():
            wait_weights(0, layer + 1)

        product = jnp.zeros((TOK, RANK), F32)
        square = jnp.zeros((TOK, 128), F32)
        for t in range(CH // TILE):
            tile = (xs[layer, :, cols(t)].astype(F32) + dot(act, wu[layer, :, cols(t)])).astype(BF16)
            xs[layer + 1, :, cols(t)] = tile
            wide_tile = tile.astype(F32)
            square += fold_lanes(wide_tile * wide_tile)
            product += dot(tile, wd[after, cols(t), :])
        return send_product(1 - slot, product, square)

    own_row = lax.fori_loop(0, LAYERS, forward, own_row)

    value_acc = jnp.zeros((TOK, 128), F32)
    for t in range(CH // TILE):
        weight = vw_ref[pl.ds(z, 1), cols(t)]
        value_acc += fold_lanes(xs[LAYERS, :, cols(t)].astype(F32) * weight)
    value_row = row_sums(value_acc)
    target_row = tv_ref[0:1, :]
    snd[0, 0:16, 0:128] = pack_rows([own_row, value_row, target_row])
    finish(exchange(0, 16))
    ssq = row_total(0, 0, own_row)
    raw = row_total(0, 3, value_row)
    target = row_total(0, 6, target_row)
    scale = lax.rsqrt(ssq * (1.0 / FEAT) + 1e-05)
    value = scale * raw
    resid = value - target
    on_weight = column(scale * resid)
    on_x = column(-scale * scale * resid * value * (1.0 / FEAT))
    product = jnp.zeros((TOK, RANK), F32)
    for t in range(CH // TILE):
        weight = vw_ref[pl.ds(z, 1), cols(t)]
        tile = (
            wide(on_weight, TILE) * weight + wide(on_x, TILE) * xs[LAYERS, :, cols(t)].astype(F32)
        ).astype(BF16)
        gx[0, :, cols(t)] = tile
        product += dot_nt(tile, wu[LAYERS - 1, :, cols(t)])
    mine[...] = product
    snd[1, 16 : 16 + TOK] = product.astype(BF16)

    def out_copy(layer, slot):
        return pltpu.make_async_copy(gbuf.at[slot], out_hbm.at[layer], gsem.at[slot])

    def backward(step, carry):
        layer = LAYERS - 1 - step
        slot = lax.rem(step + 1, 2)
        now = lax.rem(step, 2)
        finish(exchange(slot, 16 + TOK))
        total = mine[...]
        for i in range(ZN - 1):
            total = total + rcv[slot, i, 16 : 16 + TOK].astype(F32)
        pre = pre_s[layer]
        scale = scale_s[layer]
        sigma = 1.0 / (1.0 + jnp.exp(-pre))
        grad_pre = (total * sigma * (1.0 + pre * (1.0 - sigma))).astype(BF16)
        grad_f = grad_pre.astype(F32)
        inner = jnp.sum(grad_f * pre, axis=1, keepdims=True) * (1.0 / FEAT)
        scaled = (grad_f * wide(scale, RANK)).astype(BF16)
        on_x = wide(scale * scale * inner, TILE)
        on_q = wide(scale, TILE)
        below = jnp.maximum(layer - 1, 0)
        product = jnp.zeros((TOK, RANK), F32)
        for t in range(CH // TILE):
            q = dot_nt(grad_pre, wd[layer, cols(t), :])
            tile = (
                gx[now, :, cols(t)].astype(F32) + on_q * q - on_x * xs[layer, :, cols(t)].astype(F32)
            ).astype(BF16)
            gx[1 - now, :, cols(t)] = tile
            product += dot_nt(tile, wu[below, :, cols(t)])
        mine[...] = product
        snd[1 - slot, 16 : 16 + TOK] = product.astype(BF16)

        @pl.when(step >= 2)
        def _():
            out_copy(layer + 2, now).wait()

        act = act_s[layer]
        for t in range(CH // TILE):
            gbuf[now, 0:RANK, cols(t)] = dot_tn(scaled, xs[layer, :, cols(t)]).astype(BF16)
            gbuf[now, RANK : 2 * RANK, cols(t)] = dot_tn(act, gx[now, :, cols(t)]).astype(BF16)
        out_copy(layer, now).start()
        return carry

    lax.fori_loop(0, LAYERS, backward, 0)
    out_copy(1, 0).wait()
    out_copy(0, 1).wait()


def shards(inputs, targets, adapter_down, adapter_up, value_weight, returns):
    dp = lax.axis_index("dp")
    pipe = lax.axis_index("pipe")
    z = dp // 4
    xl, y = pipe // 4, pipe % 4
    down = lax.dynamic_slice_in_dim(adapter_down[0], z * CH, CH, 0)
    up = lax.dynamic_slice_in_dim(adapter_up[0], z * CH, CH, 1)
    wd = lax.all_gather(down, "pipe")
    wu = lax.all_gather(up, "pipe")
    mine = lax.dynamic_slice(targets, (y, xl * OWN), (1, OWN))
    agents = jnp.arange(returns.shape[0], dtype=jnp.int32)
    values = jnp.sum(jnp.where(mine[0][:, None] == agents, returns, 0.0), axis=-1)
    tv = lax.dynamic_update_slice(jnp.zeros((8, 128), F32), values[None], (0, z * OWN))
    any_spec = pl.BlockSpec(memory_space=pl.ANY)
    vmem = pl.BlockSpec(memory_space=pltpu.VMEM)
    part = pl.pallas_call(
        kernel,
        out_shape=jax.ShapeDtypeStruct((LAYERS, 2 * RANK, CH), BF16),
        in_specs=[any_spec, any_spec, any_spec, vmem, vmem],
        out_specs=any_spec,
        scratch_shapes=[
            pltpu.VMEM((LAYERS + 1, TOK, CH), BF16),
            pltpu.VMEM((LAYERS, CH, RANK), BF16),
            pltpu.VMEM((LAYERS, RANK, CH), BF16),
            pltpu.VMEM((2, 16 + TOK, RANK), BF16),
            pltpu.VMEM((2, ZN - 1, 16 + TOK, RANK), BF16),
            pltpu.VMEM((TOK, RANK), F32),
            pltpu.VMEM((2, TOK, CH), BF16),
            pltpu.VMEM((LAYERS, TOK, RANK), F32),
            pltpu.VMEM((LAYERS, TOK, RANK), BF16),
            pltpu.VMEM((LAYERS, TOK, 128), F32),
            pltpu.VMEM((2, 2 * RANK, CH), BF16),
            pltpu.SemaphoreType.DMA((ZN - 1,)),
            pltpu.SemaphoreType.DMA((ZN - 1,)),
            pltpu.SemaphoreType.DMA,
            pltpu.SemaphoreType.DMA((2, LAYERS)),
            pltpu.SemaphoreType.DMA((2, ZN - 1)),
            pltpu.SemaphoreType.DMA((2, ZN - 1)),
            pltpu.SemaphoreType.DMA((2,)),
        ],
        compiler_params=pltpu.CompilerParams(
            collective_id=0, has_side_effects=True, vmem_limit_bytes=56 * 1024 * 1024
        ),
        name="relay",
    )(inputs, wd, wu, value_weight.reshape(ZN, CH), tv)
    mine = lax.psum_scatter(part, "pipe", scatter_dimension=0, tiled=True)[0]
    groups = [[4 * i + j for j in range(4)] for i in range(ZN)]
    mine = lax.psum_scatter(mine, "dp", scatter_dimension=1, tiled=True, axis_index_groups=groups)
    mine = mine.astype(F32)
    return (mine[:RANK].T[None], mine[RANK:][None])


def solution(mesh):
    return jax.shard_map(
        shards,
        mesh=mesh,
        in_specs=(
            P(None, "dp", None),
            P(None, "dp"),
            P("pipe", None, None),
            P("pipe", None, None),
            P(),
            P(),
        ),
        out_specs=(P("pipe", "dp", None), P("pipe", None, "dp")),
        check_vma=False,
    )
```

```python
import functools

import jax
import jax.numpy as jnp
from jax import lax
from jax.experimental import pallas as pl
from jax.experimental.pallas import tpu as pltpu
from jax.sharding import PartitionSpec as P

LAYERS = 8
ZN = 4
TOK = 128
OWN = TOK // ZN
CH = 2048
RANK = 256
FEAT = 8192
TILE = 512
F32 = jnp.float32
BF16 = jnp.bfloat16
MESH = pl.DeviceIdType.MESH


def split3(row):
    hi = row.astype(BF16)
    rest = row - hi.astype(F32)
    mid = rest.astype(BF16)
    lo = (rest - mid.astype(F32)).astype(BF16)
    return [hi.astype(F32), mid.astype(F32), lo.astype(F32)]


def pack_rows(rows):
    parts = []
    for row in rows:
        parts += split3(row)
    at = lax.broadcasted_iota(jnp.int32, (16, 128), 0)
    tile = jnp.zeros((16, 128), F32)
    for i, part in enumerate(parts):
        tile = jnp.where(at == i, jnp.broadcast_to(part, (16, 128)), tile)
    return tile.astype(BF16)


def column(row):
    return jnp.transpose(jnp.broadcast_to(row, (TOK, 128)))


def row_sums(acc):
    return jnp.sum(jnp.transpose(acc), axis=0, keepdims=True)


def fold_lanes(tile):
    total = tile[:, 0:128]
    for i in range(1, tile.shape[1] // 128):
        total = total + tile[:, 128 * i : 128 * (i + 1)]
    return total


def wide(col, width):
    return jnp.concatenate([col] * (width // 128), axis=1)


def dot(a, b):
    return lax.dot_general(a, b, (((1,), (0,)), ((), ())), preferred_element_type=F32)


def dot_nt(a, b):
    return lax.dot_general(a, b, (((1,), (1,)), ((), ())), preferred_element_type=F32)


def dot_tn(a, b):
    return lax.dot_general(a, b, (((0,), (0,)), ((), ())), preferred_element_type=F32)


def kernel(
    x_hbm, wd_hbm, wu_hbm, vw_ref, tv_ref, out_ref,
    xs, wd, wu, snd, rcv, mine, gx, pre_s, act_s, scale_s,
    gbuf, cbuf, dsum, usum, d1, u1, d2s, u2s, d2, u2, d3s, u3s, res,
    x_ssem, x_rsem, lsem, wsem, ssem, rsem,
    y_ssem, y_rsem, n_ssem, n_rsem, c_ssem, c_rsem,
    gc_ssem, gc_rsem, g1_ssem, g1_rsem, g2_ssem, g2_rsem, g3_ssem, g3_rsem,
):
    dp = lax.axis_index("dp")
    pipe = lax.axis_index("pipe")
    z = dp // 4
    c = lax.rem(dp, 2)
    xh = lax.rem(dp // 2, 2)
    rest = lax.rem(dp, 4)
    xl = pipe // 4
    y = lax.rem(pipe, 4)
    x = xh * 2 + xl
    zs = [lax.rem(z + i, ZN) for i in range(1, ZN)]
    peers = [(zz * 4 + rest, pipe) for zz in zs]
    core_peer = (dp + 1 - 2 * c, pipe)

    def x_dev(xx):
        return (z * 4 + (xx // 2) * 2 + c, lax.rem(xx, 2) * 4 + y)

    def y_dev(yy):
        return (dp, xl * 4 + yy)

    x_at = [lax.rem(x + i, 4) for i in range(1, 4)]
    y_at = [lax.rem(y + i, 4) for i in range(1, 4)]

    def remote(src, dst, send, recv, device):
        return pltpu.make_async_remote_copy(
            src_ref=src, dst_ref=dst, send_sem=send, recv_sem=recv,
            device_id=device, device_id_type=MESH,
        )

    feats = pl.ds(pl.multiple_of(z * CH, CH), CH)
    own_down = pltpu.make_async_copy(wd_hbm.at[0, feats, :], wd.at[pipe], wsem.at[0])
    own_up = pltpu.make_async_copy(wu_hbm.at[0, :, feats], wu.at[pipe], wsem.at[1])
    own_down.start()
    own_up.start()

    def piece(zz):
        return x_hbm.at[y, pl.ds(pl.multiple_of(xl * OWN, OWN), OWN), pl.ds(pl.multiple_of(zz * CH, CH), CH)]

    own_rows = pl.ds(pl.multiple_of(z * OWN, OWN), OWN)
    own = pltpu.make_async_copy(piece(z), xs.at[0, own_rows], lsem)
    own.start()

    barrier = pltpu.get_barrier_semaphore()
    greet = peers + [core_peer, x_dev(x_at[0]), x_dev(x_at[1]), x_dev(x_at[2])]
    greet += [(dp, lax.rem(pipe + i, LAYERS)) for i in range(1, LAYERS)]
    for device in greet:
        pl.semaphore_signal(barrier, inc=1, device_id=device, device_id_type=MESH)
    pl.semaphore_wait(barrier, len(greet))

    HALF = CH // 2
    QUART = CH // 4

    def y_copy(which, i, layer):
        at = pl.ds(pl.multiple_of(c * HALF, HALF), HALF)
        far = pl.ds(pl.multiple_of(z * CH + c * HALF, HALF), HALF)
        if which == 0:
            src, dst = wd_hbm.at[0, far, :], wd.at[layer, at, :]
        else:
            src, dst = wu_hbm.at[0, :, far], wu.at[layer, :, at]
        return remote(src, dst, y_ssem.at[which, i], y_rsem.at[which, layer], y_dev(y_at[i]))

    def n_copy(which, layer, h):
        at = pl.ds(pl.multiple_of(c * HALF + h * QUART, QUART), QUART)
        ref = wd.at[layer, at, :] if which == 0 else wu.at[layer, :, at]
        return remote(ref, ref, n_ssem.at[which, layer, h], n_rsem.at[which, layer, h], x_dev(x_at[2 * h]))

    def c_copy(which, layer):
        at = pl.ds(pl.multiple_of(c * HALF, HALF), HALF)
        ref = wd.at[layer, at, :] if which == 0 else wu.at[layer, :, at]
        return remote(ref, ref, c_ssem.at[which, layer], c_rsem.at[which, layer], core_peer)

    copies = []
    for i in range(ZN - 1):
        copy = remote(piece(zs[i]), xs.at[0, own_rows], x_ssem.at[i], x_rsem.at[i], peers[i])
        copy.start()
        copies.append(copy)
    for which in (0, 1):
        for i in (0, 2, 1):
            y_copy(which, i, pipe).start()

    def pass_on(which, layer):
        in_column = layer // 4 == xl
        is_own = layer == pipe

        @pl.when(is_own)
        def _():
            (own_down if which == 0 else own_up).wait()

        @pl.when(in_column & jnp.logical_not(is_own))
        def _():
            y_copy(which, 0, layer).wait_recv()

        @pl.when(in_column)
        def _():
            n_copy(which, layer, 0).start()
            n_copy(which, layer, 1).start()

        @pl.when(jnp.logical_not(in_column))
        def _():
            n_copy(which, layer, 0).wait_recv()
            n_copy(which, layer, 1).wait_recv()

        @pl.when(jnp.logical_not(is_own))
        def _():
            c_copy(which, layer).start()

    def wait_weights(which, layer):
        @pl.when(layer != pipe)
        def _():
            c_copy(which, layer).wait_recv()

    def sent_weights(which, layer):
        @pl.when(layer // 4 == xl)
        def _():
            n_copy(which, layer, 0).wait_send()
            n_copy(which, layer, 1).wait_send()

        @pl.when(layer != pipe)
        def _():
            c_copy(which, layer).wait_send()

    def exchange(slot, rows):
        return [
            remote(
                snd.at[slot, pl.ds(0, rows)], rcv.at[slot, i, pl.ds(0, rows)],
                ssem.at[slot, i], rsem.at[slot, i], peers[i],
            )
            for i in range(ZN - 1)
        ]

    def begin(copies):
        for copy in copies:
            copy.start()

    def finish(copies):
        for copy in copies:
            copy.wait()

    def cols(t):
        return slice(t * TILE, (t + 1) * TILE)

    def send_product(slot, product, square):
        mine[...] = product
        snd[slot, 16 : 16 + TOK] = product.astype(BF16)
        row = row_sums(square)
        snd[slot, 0:16, 0:128] = pack_rows([row])
        return row

    def row_total(slot, first, own_row):
        total = own_row
        for i in range(ZN - 1):
            part = rcv[slot, i, 0:16, 0:128].astype(F32)[first : first + 3]
            total = total + jnp.sum(part, axis=0, keepdims=True)
        return total

    snd[...] = jnp.zeros_like(snd)
    own.wait()
    finish(copies)
    pass_on(0, 0)
    wait_weights(0, 0)
    product = jnp.zeros((TOK, RANK), F32)
    square = jnp.zeros((TOK, 128), F32)
    for t in range(CH // TILE):
        tile = xs[0, :, cols(t)]
        wide_tile = tile.astype(F32)
        square += fold_lanes(wide_tile * wide_tile)
        product += dot(tile, wd[0, cols(t), :])
    own_row = send_product(0, product, square)
    pass_on(1, 0)
    pass_on(0, 1)

    def forward(layer, own_row):
        slot = lax.rem(layer, 2)
        begin(exchange(slot, 16 + TOK))

        @pl.when(layer < LAYERS - 1)
        def _():
            pass_on(1, layer + 1)

        @pl.when(layer < LAYERS - 2)
        def _():
            pass_on(0, layer + 2)

        finish(exchange(slot, 16 + TOK))
        total = mine[...]
        for i in range(ZN - 1):
            total = total + rcv[slot, i, 16 : 16 + TOK].astype(F32)
        ssq = row_total(slot, 0, own_row)
        scale = column(lax.rsqrt(ssq * (1.0 / FEAT) + 1e-05))
        pre = total * wide(scale, RANK)
        act = (pre / (1.0 + jnp.exp(-pre))).astype(BF16)
        scale_s[layer] = scale
        pre_s[layer] = pre
        act_s[layer] = act
        after = jnp.minimum(layer + 1, LAYERS - 1)
        wait_weights(1, layer)

        @pl.when(layer < LAYERS - 1)
        def _():
            wait_weights(0, layer + 1)

        product = jnp.zeros((TOK, RANK), F32)
        square = jnp.zeros((TOK, 128), F32)
        for t in range(CH // TILE):
            tile = (xs[layer, :, cols(t)].astype(F32) + dot(act, wu[layer, :, cols(t)])).astype(BF16)
            xs[layer + 1, :, cols(t)] = tile
            wide_tile = tile.astype(F32)
            square += fold_lanes(wide_tile * wide_tile)
            product += dot(tile, wd[after, cols(t), :])
        return send_product(1 - slot, product, square)

    own_row = lax.fori_loop(0, LAYERS, forward, own_row)

    value_acc = jnp.zeros((TOK, 128), F32)
    for t in range(CH // TILE):
        weight = vw_ref[pl.ds(z, 1), cols(t)]
        value_acc += fold_lanes(xs[LAYERS, :, cols(t)].astype(F32) * weight)
    value_row = row_sums(value_acc)
    target_row = tv_ref[0:1, :]
    snd[0, 0:16, 0:128] = pack_rows([own_row, value_row, target_row])
    begin(exchange(0, 16))
    for which in (0, 1):
        for i in range(3):
            y_copy(which, i, pipe).wait_send()
        for layer in range(LAYERS):
            sent_weights(which, layer)
    finish(exchange(0, 16))
    ssq = row_total(0, 0, own_row)
    raw = row_total(0, 3, value_row)
    target = row_total(0, 6, target_row)
    scale = lax.rsqrt(ssq * (1.0 / FEAT) + 1e-05)
    value = scale * raw
    resid = value - target
    on_weight = column(scale * resid)
    on_x = column(-scale * scale * resid * value * (1.0 / FEAT))
    product = jnp.zeros((TOK, RANK), F32)
    for t in range(CH // TILE):
        weight = vw_ref[pl.ds(z, 1), cols(t)]
        tile = (
            wide(on_weight, TILE) * weight + wide(on_x, TILE) * xs[LAYERS, :, cols(t)].astype(F32)
        ).astype(BF16)
        gx[0, :, cols(t)] = tile
        product += dot_nt(tile, wu[LAYERS - 1, :, cols(t)])
    mine[...] = product
    snd[1, 16 : 16 + TOK] = product.astype(BF16)
    begin(exchange(1, 16 + TOK))

    def core_copy(layer, half):
        slot = lax.rem(layer, 2)
        return remote(
            gbuf.at[slot, 2 * half + 1 - c], cbuf.at[layer, half],
            gc_ssem.at[slot, half], gc_rsem.at[layer, half], core_peer,
        )

    def first_copies(layer):
        slot = lax.rem(layer, 2)
        found = []
        for i in range(3):
            found.append(remote(
                dsum.at[slot, x_at[i]], d1.at[layer, i],
                g1_ssem.at[slot, 0, i], g1_rsem.at[layer, 0, i], x_dev(x_at[i]),
            ))
            found.append(remote(
                usum.at[slot, y_at[i]], u1.at[layer, i],
                g1_ssem.at[slot, 1, i], g1_rsem.at[layer, 1, i], y_dev(y_at[i]),
            ))
        return found

    def second_copies(layer):
        slot = lax.rem(layer, 2)
        found = []
        for i in range(3):
            found.append(remote(
                d2s.at[slot, y_at[i]], d2.at[layer, i],
                g2_ssem.at[slot, 0, i], g2_rsem.at[layer, 0, i], y_dev(y_at[i]),
            ))
            found.append(remote(
                u2s.at[slot, x_at[i]], u2.at[layer, i],
                g2_ssem.at[slot, 1, i], g2_rsem.at[layer, 1, i], x_dev(x_at[i]),
            ))
        return found

    def last_copies(layer):
        return [
            remote(src.at[layer], res.at[which, pipe], g3_ssem.at[layer, which], g3_rsem.at[which, pipe], (dp, layer))
            for which, src in ((0, d3s), (1, u3s))
        ]

    def add_cores(layer):
        slot = lax.rem(layer, 2)
        for half in (0, 1):
            core_copy(layer, half).wait()
        for half in (0, 1):
            for block in range(2):
                for part in range(4):
                    at = slice(block * 128 + part * 32, block * 128 + part * 32 + 32)
                    dsum[slot, 2 * half + block, part] = (
                        gbuf[slot, 2 * half + c, at].astype(F32) + cbuf[layer, half, at].astype(F32)
                    ).astype(BF16)
                    at = slice(RANK + at.start, RANK + at.stop)
                    usum[slot, part, 2 * half + block] = (
                        gbuf[slot, 2 * half + c, at].astype(F32) + cbuf[layer, half, at].astype(F32)
                    ).astype(BF16)
        begin(first_copies(layer))

    def add_first(layer):
        slot = lax.rem(layer, 2)
        finish(first_copies(layer))
        for part in range(4):
            for total, at, got, to in ((dsum, x, d1, d2s), (usum, y, u1, u2s)):
                value = total[slot, at, part].astype(F32)
                for i in range(3):
                    value = value + got[layer, i, part].astype(F32)
                to[slot, part] = value.astype(BF16)
        begin(second_copies(layer))

    def add_second(layer):
        slot = lax.rem(layer, 2)
        finish(second_copies(layer))
        done = []
        for total, at, got in ((d2s, y, d2), (u2s, x, u2)):
            value = total[slot, at].astype(F32)
            for i in range(3):
                value = value + got[layer, i].astype(F32)
            done.append(value.astype(BF16))

        @pl.when(layer == pipe)
        def _():
            res[0, pipe] = done[0]
            res[1, pipe] = done[1]

        @pl.when(layer != pipe)
        def _():
            d3s[layer] = done[0]
            u3s[layer] = done[1]
            begin(last_copies(layer))

    def sums(step):
        @pl.when((step >= 1) & (step < LAYERS + 1))
        def _():
            add_cores(LAYERS - step)

        @pl.when((step >= 2) & (step < LAYERS + 2))
        def _():
            add_first(LAYERS + 1 - step)

        @pl.when(step >= 3)
        def _():
            add_second(LAYERS + 2 - step)

    def backward(step, carry):
        layer = LAYERS - 1 - step
        slot = lax.rem(step + 1, 2)
        now = lax.rem(step, 2)
        finish(exchange(slot, 16 + TOK))
        total = mine[...]
        for i in range(ZN - 1):
            total = total + rcv[slot, i, 16 : 16 + TOK].astype(F32)
        pre = pre_s[layer]
        scale = scale_s[layer]
        sigma = 1.0 / (1.0 + jnp.exp(-pre))
        grad_pre = (total * sigma * (1.0 + pre * (1.0 - sigma))).astype(BF16)
        grad_f = grad_pre.astype(F32)
        inner = jnp.sum(grad_f * pre, axis=1, keepdims=True) * (1.0 / FEAT)
        scaled = (grad_f * wide(scale, RANK)).astype(BF16)

        @pl.when(layer > 0)
        def _():
            on_x = wide(scale * scale * inner, TILE)
            on_q = wide(scale, TILE)
            product = jnp.zeros((TOK, RANK), F32)
            for t in range(CH // TILE):
                q = dot_nt(grad_pre, wd[layer, cols(t), :])
                tile = (
                    gx[now, :, cols(t)].astype(F32) + on_q * q - on_x * xs[layer, :, cols(t)].astype(F32)
                ).astype(BF16)
                gx[1 - now, :, cols(t)] = tile
                product += dot_nt(tile, wu[layer - 1, :, cols(t)])
            mine[...] = product
            snd[1 - slot, 16 : 16 + TOK] = product.astype(BF16)
            begin(exchange(1 - slot, 16 + TOK))

        act = act_s[layer]
        turn = lax.rem(layer, 2)
        for t in range(CH // TILE):
            gbuf[turn, t, 0:RANK] = dot_tn(scaled, xs[layer, :, cols(t)]).astype(BF16)
            gbuf[turn, t, RANK : 2 * RANK] = dot_tn(act, gx[now, :, cols(t)]).astype(BF16)
        for half in (0, 1):
            core_copy(layer, half).start()
        sums(step)
        return carry

    lax.fori_loop(0, LAYERS, backward, 0)

    def rest_of_sums(step, carry):
        sums(step)
        return carry

    lax.fori_loop(LAYERS, LAYERS + 3, rest_of_sums, 0)

    def finish_last(layer, carry):
        @pl.when(layer != pipe)
        def _():
            for copy in last_copies(layer):
                copy.wait_send()
            for which in (0, 1):
                remote(
                    d3s.at[layer], res.at[which, layer],
                    g3_ssem.at[layer, which], g3_rsem.at[which, layer], (dp, layer),
                ).wait_recv()
        return carry

    lax.fori_loop(0, LAYERS, finish_last, 0)
    for which in (0, 1):
        for part in range(LAYERS):
            out_ref[which, part * 32 : part * 32 + 32] = res[which, part]


def shards(inputs, targets, adapter_down, adapter_up, value_weight, returns):
    dp = lax.axis_index("dp")
    pipe = lax.axis_index("pipe")
    z = dp // 4
    xl, y = pipe // 4, pipe % 4
    mine = lax.dynamic_slice(targets, (y, xl * OWN), (1, OWN))
    agents = jnp.arange(returns.shape[0], dtype=jnp.int32)
    values = jnp.sum(jnp.where(mine[0][:, None] == agents, returns, 0.0), axis=-1)
    tv = lax.dynamic_update_slice(jnp.zeros((8, 128), F32), values[None], (0, z * OWN))
    any_spec = pl.BlockSpec(memory_space=pl.ANY)
    vmem = pl.BlockSpec(memory_space=pltpu.VMEM)
    dma = pltpu.SemaphoreType.DMA
    part = pl.pallas_call(
        kernel,
        out_shape=jax.ShapeDtypeStruct((2, RANK, TILE), BF16),
        in_specs=[any_spec, any_spec, any_spec, vmem, vmem],
        out_specs=vmem,
        scratch_shapes=[
            pltpu.VMEM((LAYERS + 1, TOK, CH), BF16),
            pltpu.VMEM((LAYERS, CH, RANK), BF16),
            pltpu.VMEM((LAYERS, RANK, CH), BF16),
            pltpu.VMEM((2, 16 + TOK, RANK), BF16),
            pltpu.VMEM((2, ZN - 1, 16 + TOK, RANK), BF16),
            pltpu.VMEM((TOK, RANK), F32),
            pltpu.VMEM((2, TOK, CH), BF16),
            pltpu.VMEM((LAYERS, TOK, RANK), F32),
            pltpu.VMEM((LAYERS, TOK, RANK), BF16),
            pltpu.VMEM((LAYERS, TOK, 128), F32),
            pltpu.VMEM((2, 4, 2 * RANK, TILE), BF16),
            pltpu.VMEM((LAYERS, 2, 2 * RANK, TILE), BF16),
            pltpu.VMEM((2, 4, 4, 32, TILE), BF16),
            pltpu.VMEM((2, 4, 4, 32, TILE), BF16),
            pltpu.VMEM((LAYERS, 3, 4, 32, TILE), BF16),
            pltpu.VMEM((LAYERS, 3, 4, 32, TILE), BF16),
            pltpu.VMEM((2, 4, 32, TILE), BF16),
            pltpu.VMEM((2, 4, 32, TILE), BF16),
            pltpu.VMEM((LAYERS, 3, 32, TILE), BF16),
            pltpu.VMEM((LAYERS, 3, 32, TILE), BF16),
            pltpu.VMEM((LAYERS, 32, TILE), BF16),
            pltpu.VMEM((LAYERS, 32, TILE), BF16),
            pltpu.VMEM((2, LAYERS, 32, TILE), BF16),
            dma((ZN - 1,)),
            dma((ZN - 1,)),
            dma,
            dma((2,)),
            dma((2, ZN - 1)),
            dma((2, ZN - 1)),
            dma((2, 3)),
            dma((2, LAYERS)),
            dma((2, LAYERS, 2)),
            dma((2, LAYERS, 2)),
            dma((2, LAYERS)),
            dma((2, LAYERS)),
            dma((2, 2)),
            dma((LAYERS, 2)),
            dma((2, 2, 3)),
            dma((LAYERS, 2, 3)),
            dma((2, 2, 3)),
            dma((LAYERS, 2, 3)),
            dma((LAYERS, 2)),
            dma((2, LAYERS)),
        ],
        compiler_params=pltpu.CompilerParams(
            collective_id=0, has_side_effects=True, vmem_limit_bytes=60 * 1024 * 1024
        ),
        name="relay",
    )(inputs, adapter_down, adapter_up, value_weight.reshape(ZN, CH), tv)
    mine = part.astype(F32)
    return (mine[0].T[None], mine[1][None])


def solution(mesh):
    return jax.shard_map(
        shards,
        mesh=mesh,
        in_specs=(
            P(None, "dp", None),
            P(None, "dp"),
            P("pipe", None, None),
            P("pipe", None, None),
            P(),
            P(),
        ),
        out_specs=(P("pipe", "dp", None), P("pipe", None, "dp")),
        check_vma=False,
    )
```

```python
import functools

import jax
import jax.numpy as jnp
from jax import lax
from jax.experimental import pallas as pl
from jax.experimental.pallas import tpu as pltpu
from jax.sharding import PartitionSpec as P

LAYERS = 8
ZN = 4
TOK = 128
OWN = TOK // ZN
CH = 2048
RANK = 256
FEAT = 8192
TILE = 512
F32 = jnp.float32
BF16 = jnp.bfloat16
MESH = pl.DeviceIdType.MESH


def split3(row):
    hi = row.astype(BF16)
    rest = row - hi.astype(F32)
    mid = rest.astype(BF16)
    lo = (rest - mid.astype(F32)).astype(BF16)
    return [hi.astype(F32), mid.astype(F32), lo.astype(F32)]


def pack_rows(rows):
    parts = []
    for row in rows:
        parts += split3(row)
    at = lax.broadcasted_iota(jnp.int32, (16, 128), 0)
    tile = jnp.zeros((16, 128), F32)
    for i, part in enumerate(parts):
        tile = jnp.where(at == i, jnp.broadcast_to(part, (16, 128)), tile)
    return tile.astype(BF16)


def column(row):
    return jnp.transpose(jnp.broadcast_to(row, (TOK, 128)))


def row_sums(acc):
    return jnp.sum(jnp.transpose(acc), axis=0, keepdims=True)


def fold_lanes(tile):
    total = tile[:, 0:128]
    for i in range(1, tile.shape[1] // 128):
        total = total + tile[:, 128 * i : 128 * (i + 1)]
    return total


def wide(col, width):
    return jnp.concatenate([col] * (width // 128), axis=1)


def dot(a, b):
    return lax.dot_general(a, b, (((1,), (0,)), ((), ())), preferred_element_type=F32)


def dot_nt(a, b):
    return lax.dot_general(a, b, (((1,), (1,)), ((), ())), preferred_element_type=F32)


def dot_tn(a, b):
    return lax.dot_general(a, b, (((0,), (0,)), ((), ())), preferred_element_type=F32)


def kernel(
    x_hbm, wd_hbm, wu_hbm, vw_hbm, ret_hbm, targets_ref, out_ref,
    vw_s, ret_s,
    xs, wd, wu, snd, rcv, mine, gx, pre_s, act_s, scale_s,
    gbuf, cbuf, dsum, usum, d1, u1, d2s, u2s, d2, u2, d3s, u3s, res,
    x_ssem, x_rsem, lsem, wsem, ssem, rsem,
    y_ssem, y_rsem, r_ssem, r_rsem, vsem, n_ssem, n_rsem, c_ssem, c_rsem,
    gc_ssem, gc_rsem, g1_ssem, g1_rsem, g2_ssem, g2_rsem, g3_ssem, g3_rsem,
):
    dp = lax.axis_index("dp")
    pipe = lax.axis_index("pipe")
    z = dp // 4
    c = lax.rem(dp, 2)
    xh = lax.rem(dp // 2, 2)
    rest = lax.rem(dp, 4)
    xl = pipe // 4
    y = lax.rem(pipe, 4)
    x = xh * 2 + xl
    zs = [lax.rem(z + i, ZN) for i in range(1, ZN)]
    peers = [(zz * 4 + rest, pipe) for zz in zs]
    core_peer = (dp + 1 - 2 * c, pipe)

    def x_dev(xx):
        return (z * 4 + (xx // 2) * 2 + c, lax.rem(xx, 2) * 4 + y)

    def y_dev(yy):
        return (dp, xl * 4 + yy)

    x_at = [lax.rem(x + i, 4) for i in range(1, 4)]
    y_at = [lax.rem(y + i, 4) for i in range(1, 4)]

    def remote(src, dst, send, recv, device):
        return pltpu.make_async_remote_copy(
            src_ref=src, dst_ref=dst, send_sem=send, recv_sem=recv,
            device_id=device, device_id_type=MESH,
        )

    feats = pl.ds(pl.multiple_of(z * CH, CH), CH)
    own_down = pltpu.make_async_copy(wd_hbm.at[0, feats, :], wd.at[pipe], wsem.at[0])
    own_up = pltpu.make_async_copy(wu_hbm.at[0, :, feats], wu.at[pipe], wsem.at[1])
    own_down.start()
    own_up.start()

    def piece(zz):
        return x_hbm.at[y, pl.ds(pl.multiple_of(xl * OWN, OWN), OWN), pl.ds(pl.multiple_of(zz * CH, CH), CH)]

    own_rows = pl.ds(pl.multiple_of(z * OWN, OWN), OWN)
    own = pltpu.make_async_copy(piece(z), xs.at[0, own_rows], lsem)
    own.start()
    small = pltpu.make_async_copy(vw_hbm.at[feats], vw_s.at[0], vsem.at[4])
    small.start()
    ret_copies = [
        pltpu.make_async_copy(ret_hbm.at[pl.ds(128 * i, 128)], ret_s.at[i], vsem.at[i]) for i in range(4)
    ]
    for copy in ret_copies:
        copy.start()

    barrier = pltpu.get_barrier_semaphore()
    greet = peers + [core_peer, x_dev(x_at[0]), x_dev(x_at[1]), x_dev(x_at[2])]
    greet += [(dp, lax.rem(pipe + i, LAYERS)) for i in range(1, LAYERS)]
    for device in greet:
        pl.semaphore_signal(barrier, inc=1, device_id=device, device_id_type=MESH)
    pl.semaphore_wait(barrier, len(greet))

    HALF = CH // 2
    QUART = CH // 4

    def y_copy(which, i, layer):
        at = pl.ds(pl.multiple_of(c * HALF, HALF), HALF)
        far = pl.ds(pl.multiple_of(z * CH + c * HALF, HALF), HALF)
        if which == 0:
            src, dst = wd_hbm.at[0, far, :], wd.at[layer, at, :]
        else:
            src, dst = wu_hbm.at[0, :, far], wu.at[layer, :, at]
        return remote(src, dst, y_ssem.at[which, i], y_rsem.at[which, layer], y_dev(y_at[i]))

    def quarter(which, layer, h):
        at = pl.ds(pl.multiple_of(c * HALF + h * QUART, QUART), QUART)
        return wd.at[layer, at, :] if which == 0 else wu.at[layer, :, at]

    def r_copy(which, layer, h):
        ref = quarter(which, layer, h)
        return remote(ref, ref, r_ssem.at[which, h], r_rsem.at[which, h], y_dev(y_at[2 * h]))

    def n_copy(which, layer, h):
        ref = quarter(which, layer, h)
        return remote(ref, ref, n_ssem.at[which, layer, h], n_rsem.at[which, layer, h], x_dev(x_at[2 * h]))

    def c_copy(which, layer):
        at = pl.ds(pl.multiple_of(c * HALF, HALF), HALF)
        ref = wd.at[layer, at, :] if which == 0 else wu.at[layer, :, at]
        return remote(ref, ref, c_ssem.at[which, layer], c_rsem.at[which, layer], core_peer)

    copies = []
    for i in range(ZN - 1):
        copy = remote(piece(zs[i]), xs.at[0, own_rows], x_ssem.at[i], x_rsem.at[i], peers[i])
        copy.start()
        copies.append(copy)
    for which in (0, 1):
        for i in (0, 2):
            y_copy(which, i, pipe).start()
        (own_down if which == 0 else own_up).wait()
        for h in (0, 1):
            n_copy(which, pipe, h).start()

    def column_layer(i):
        return xl * 4 + y_at[i]

    def spread(which):
        for i, h in ((2, 0), (0, 1)):
            layer = column_layer(i)
            y_copy(which, 0, layer).wait_recv()
            r_copy(which, layer, h).start()
            c_copy(which, layer).start()
            n_copy(which, layer, 0).start()
            n_copy(which, layer, 1).start()
        layer = column_layer(1)
        for h in (0, 1):
            r_copy(which, layer, h).wait_recv()
            n_copy(which, layer, h).start()
        c_copy(which, layer).start()

    def pass_on(which, layer):
        @pl.when(layer // 4 != xl)
        def _():
            n_copy(which, layer, 0).wait_recv()
            n_copy(which, layer, 1).wait_recv()
            c_copy(which, layer).start()

    def wait_weights(which, layer):
        @pl.when(layer != pipe)
        def _():
            c_copy(which, layer).wait_recv()

    def sent_weights(which, layer):
        @pl.when(layer // 4 == xl)
        def _():
            n_copy(which, layer, 0).wait_send()
            n_copy(which, layer, 1).wait_send()

        @pl.when(layer != pipe)
        def _():
            c_copy(which, layer).wait_send()

    def exchange(slot, rows):
        return [
            remote(
                snd.at[slot, pl.ds(0, rows)], rcv.at[slot, i, pl.ds(0, rows)],
                ssem.at[slot, i], rsem.at[slot, i], peers[i],
            )
            for i in range(ZN - 1)
        ]

    def begin(copies):
        for copy in copies:
            copy.start()

    def finish(copies):
        for copy in copies:
            copy.wait()

    def cols(t):
        return slice(t * TILE, (t + 1) * TILE)

    def send_product(slot, product, square):
        mine[...] = product
        snd[slot, 16 : 16 + TOK] = product.astype(BF16)
        row = row_sums(square)
        snd[slot, 0:16, 0:128] = pack_rows([row])
        return row

    def row_total(slot, first, own_row):
        total = own_row
        for i in range(ZN - 1):
            part = rcv[slot, i, 0:16, 0:128].astype(F32)[first : first + 3]
            total = total + jnp.sum(part, axis=0, keepdims=True)
        return total

    snd[...] = jnp.zeros_like(snd)
    own.wait()
    finish(copies)
    wanted = targets_ref[pl.ds(y, 1), :].astype(F32)
    wanted = column(jnp.concatenate([wanted, jnp.zeros_like(wanted)], axis=1))
    lane = lax.broadcasted_iota(jnp.int32, (TOK, 128), 1)
    small.wait()
    for copy in ret_copies:
        copy.wait()
    found = jnp.zeros((TOK, 128), F32)
    for i in range(4):
        agent = (lane + 128 * i).astype(F32)
        found += jnp.where(wanted == agent, jnp.broadcast_to(ret_s[i : i + 1, :], (TOK, 128)), 0.0)
    target_tile = pltpu.roll(
        jnp.broadcast_to(row_sums(found), (8, 128)), lax.rem(z * OWN + 128 - xl * OWN, 128), axis=1
    )
    target_tile = jnp.where((lane[:8] >= z * OWN) & (lane[:8] < z * OWN + OWN), target_tile, 0.0)
    target_row = target_tile[0:1]
    spread(0)
    pass_on(0, 0)
    wait_weights(0, 0)
    product = jnp.zeros((TOK, RANK), F32)
    square = jnp.zeros((TOK, 128), F32)
    for t in range(CH // TILE):
        tile = xs[0, :, cols(t)]
        wide_tile = tile.astype(F32)
        square += fold_lanes(wide_tile * wide_tile)
        product += dot(tile, wd[0, cols(t), :])
    own_row = send_product(0, product, square)

    def forward(layer, own_row):
        slot = lax.rem(layer, 2)
        begin(exchange(slot, 16 + TOK))

        @pl.when(layer == 0)
        def _():
            pass_on(0, 1)
            spread(1)
            pass_on(1, 0)

        @pl.when(layer < LAYERS - 1)
        def _():
            pass_on(1, layer + 1)

        @pl.when(layer < LAYERS - 2)
        def _():
            pass_on(0, layer + 2)

        finish(exchange(slot, 16 + TOK))
        total = mine[...]
        for i in range(ZN - 1):
            total = total + rcv[slot, i, 16 : 16 + TOK].astype(F32)
        ssq = row_total(slot, 0, own_row)
        scale = column(lax.rsqrt(ssq * (1.0 / FEAT) + 1e-05))
        pre = total * wide(scale, RANK)
        act = (pre / (1.0 + jnp.exp(-pre))).astype(BF16)
        scale_s[layer] = scale
        pre_s[layer] = pre
        act_s[layer] = act
        after = jnp.minimum(layer + 1, LAYERS - 1)
        wait_weights(1, layer)

        @pl.when(layer < LAYERS - 1)
        def _():
            wait_weights(0, layer + 1)

        product = jnp.zeros((TOK, RANK), F32)
        square = jnp.zeros((TOK, 128), F32)
        for t in range(CH // TILE):
            tile = (xs[layer, :, cols(t)].astype(F32) + dot(act, wu[layer, :, cols(t)])).astype(BF16)
            xs[layer + 1, :, cols(t)] = tile
            wide_tile = tile.astype(F32)
            square += fold_lanes(wide_tile * wide_tile)
            product += dot(tile, wd[after, cols(t), :])
        return send_product(1 - slot, product, square)

    own_row = lax.fori_loop(0, LAYERS, forward, own_row)

    value_acc = jnp.zeros((TOK, 128), F32)
    for t in range(CH // TILE):
        weight = vw_s[0:1, cols(t)]
        value_acc += fold_lanes(xs[LAYERS, :, cols(t)].astype(F32) * weight)
    value_row = row_sums(value_acc)
    snd[0, 0:16, 0:128] = pack_rows([own_row, value_row, target_row])
    begin(exchange(0, 16))
    for which in (0, 1):
        for i in (0, 2):
            y_copy(which, i, pipe).wait_send()
        for h in (0, 1):
            r_copy(which, pipe, h).wait_send()
        for layer in range(LAYERS):
            sent_weights(which, layer)
    finish(exchange(0, 16))
    ssq = row_total(0, 0, own_row)
    raw = row_total(0, 3, value_row)
    target = row_total(0, 6, target_row)
    scale = lax.rsqrt(ssq * (1.0 / FEAT) + 1e-05)
    value = scale * raw
    resid = value - target
    on_weight = column(scale * resid)
    on_x = column(-scale * scale * resid * value * (1.0 / FEAT))
    product = jnp.zeros((TOK, RANK), F32)
    for t in range(CH // TILE):
        weight = vw_s[0:1, cols(t)]
        tile = (
            wide(on_weight, TILE) * weight + wide(on_x, TILE) * xs[LAYERS, :, cols(t)].astype(F32)
        ).astype(BF16)
        gx[0, :, cols(t)] = tile
        product += dot_nt(tile, wu[LAYERS - 1, :, cols(t)])
    mine[...] = product
    snd[1, 16 : 16 + TOK] = product.astype(BF16)
    begin(exchange(1, 16 + TOK))

    def core_copy(layer, half):
        slot = lax.rem(layer, 2)
        return remote(
            gbuf.at[slot, 2 * half + 1 - c], cbuf.at[layer, half],
            gc_ssem.at[slot, half], gc_rsem.at[layer, half], core_peer,
        )

    def first_copies(layer):
        slot = lax.rem(layer, 2)
        found = []
        for i in range(3):
            found.append(remote(
                dsum.at[slot, x_at[i]], d1.at[layer, i],
                g1_ssem.at[slot, 0, i], g1_rsem.at[layer, 0, i], x_dev(x_at[i]),
            ))
            found.append(remote(
                usum.at[slot, y_at[i]], u1.at[layer, i],
                g1_ssem.at[slot, 1, i], g1_rsem.at[layer, 1, i], y_dev(y_at[i]),
            ))
        return found

    def second_copies(layer):
        slot = lax.rem(layer, 2)
        found = []
        for i in range(3):
            found.append(remote(
                d2s.at[slot, y_at[i]], d2.at[layer, i],
                g2_ssem.at[slot, 0, i], g2_rsem.at[layer, 0, i], y_dev(y_at[i]),
            ))
            found.append(remote(
                u2s.at[slot, x_at[i]], u2.at[layer, i],
                g2_ssem.at[slot, 1, i], g2_rsem.at[layer, 1, i], x_dev(x_at[i]),
            ))
        return found

    def last_copies(layer):
        return [
            remote(src.at[layer], res.at[which, pipe], g3_ssem.at[layer, which], g3_rsem.at[which, pipe], (dp, layer))
            for which, src in ((0, d3s), (1, u3s))
        ]

    def add_cores(layer):
        slot = lax.rem(layer, 2)
        for half in (0, 1):
            core_copy(layer, half).wait()
        for half in (0, 1):
            for block in range(2):
                for part in range(4):
                    at = slice(block * 128 + part * 32, block * 128 + part * 32 + 32)
                    dsum[slot, 2 * half + block, part] = (
                        gbuf[slot, 2 * half + c, at].astype(F32) + cbuf[layer, half, at].astype(F32)
                    ).astype(BF16)
                    at = slice(RANK + at.start, RANK + at.stop)
                    usum[slot, part, 2 * half + block] = (
                        gbuf[slot, 2 * half + c, at].astype(F32) + cbuf[layer, half, at].astype(F32)
                    ).astype(BF16)
        begin(first_copies(layer))

    def add_first(layer):
        slot = lax.rem(layer, 2)
        finish(first_copies(layer))
        for part in range(4):
            for total, at, got, to in ((dsum, x, d1, d2s), (usum, y, u1, u2s)):
                value = total[slot, at, part].astype(F32)
                for i in range(3):
                    value = value + got[layer, i, part].astype(F32)
                to[slot, part] = value.astype(BF16)
        begin(second_copies(layer))

    def add_second(layer):
        slot = lax.rem(layer, 2)
        finish(second_copies(layer))
        done = []
        for total, at, got in ((d2s, y, d2), (u2s, x, u2)):
            value = total[slot, at].astype(F32)
            for i in range(3):
                value = value + got[layer, i].astype(F32)
            done.append(value.astype(BF16))

        @pl.when(layer == pipe)
        def _():
            res[0, pipe] = done[0]
            res[1, pipe] = done[1]

        @pl.when(layer != pipe)
        def _():
            d3s[layer] = done[0]
            u3s[layer] = done[1]
            begin(last_copies(layer))

    def sums(step):
        @pl.when((step >= 1) & (step < LAYERS + 1))
        def _():
            add_cores(LAYERS - step)

        @pl.when((step >= 2) & (step < LAYERS + 2))
        def _():
            add_first(LAYERS + 1 - step)

        @pl.when(step >= 3)
        def _():
            add_second(LAYERS + 2 - step)

    def backward(step, carry):
        layer = LAYERS - 1 - step
        slot = lax.rem(step + 1, 2)
        now = lax.rem(step, 2)
        finish(exchange(slot, 16 + TOK))
        total = mine[...]
        for i in range(ZN - 1):
            total = total + rcv[slot, i, 16 : 16 + TOK].astype(F32)
        pre = pre_s[layer]
        scale = scale_s[layer]
        sigma = 1.0 / (1.0 + jnp.exp(-pre))
        grad_pre = (total * sigma * (1.0 + pre * (1.0 - sigma))).astype(BF16)
        grad_f = grad_pre.astype(F32)
        inner = jnp.sum(grad_f * pre, axis=1, keepdims=True) * (1.0 / FEAT)
        scaled = (grad_f * wide(scale, RANK)).astype(BF16)

        @pl.when(layer > 0)
        def _():
            on_x = wide(scale * scale * inner, TILE)
            on_q = wide(scale, TILE)
            product = jnp.zeros((TOK, RANK), F32)
            for t in range(CH // TILE):
                q = dot_nt(grad_pre, wd[layer, cols(t), :])
                tile = (
                    gx[now, :, cols(t)].astype(F32) + on_q * q - on_x * xs[layer, :, cols(t)].astype(F32)
                ).astype(BF16)
                gx[1 - now, :, cols(t)] = tile
                product += dot_nt(tile, wu[layer - 1, :, cols(t)])
            mine[...] = product
            snd[1 - slot, 16 : 16 + TOK] = product.astype(BF16)
            begin(exchange(1 - slot, 16 + TOK))

        act = act_s[layer]
        turn = lax.rem(layer, 2)
        for t in range(CH // TILE):
            gbuf[turn, t, 0:RANK] = dot_tn(scaled, xs[layer, :, cols(t)]).astype(BF16)
            gbuf[turn, t, RANK : 2 * RANK] = dot_tn(act, gx[now, :, cols(t)]).astype(BF16)
        for half in (0, 1):
            core_copy(layer, half).start()
        sums(step)
        return carry

    lax.fori_loop(0, LAYERS, backward, 0)

    def rest_of_sums(step, carry):
        sums(step)
        return carry

    lax.fori_loop(LAYERS, LAYERS + 3, rest_of_sums, 0)

    def finish_last(layer, carry):
        @pl.when(layer != pipe)
        def _():
            for copy in last_copies(layer):
                copy.wait_send()
            for which in (0, 1):
                remote(
                    d3s.at[layer], res.at[which, layer],
                    g3_ssem.at[layer, which], g3_rsem.at[which, layer], (dp, layer),
                ).wait_recv()
        return carry

    lax.fori_loop(0, LAYERS, finish_last, 0)
    for which in (0, 1):
        for part in range(LAYERS):
            out_ref[which, part * 32 : part * 32 + 32] = res[which, part]


def shards(inputs, targets, adapter_down, adapter_up, value_weight, returns):
    any_spec = pl.BlockSpec(memory_space=pl.ANY)
    vmem = pl.BlockSpec(memory_space=pltpu.VMEM)
    dma = pltpu.SemaphoreType.DMA
    part = pl.pallas_call(
        kernel,
        out_shape=jax.ShapeDtypeStruct((2, RANK, TILE), BF16),
        in_specs=[any_spec, any_spec, any_spec, any_spec, any_spec, vmem],
        out_specs=vmem,
        scratch_shapes=[
            pltpu.VMEM((8, CH), F32),
            pltpu.VMEM((8, 128), F32),
            pltpu.VMEM((LAYERS + 1, TOK, CH), BF16),
            pltpu.VMEM((LAYERS, CH, RANK), BF16),
            pltpu.VMEM((LAYERS, RANK, CH), BF16),
            pltpu.VMEM((2, 16 + TOK, RANK), BF16),
            pltpu.VMEM((2, ZN - 1, 16 + TOK, RANK), BF16),
            pltpu.VMEM((TOK, RANK), F32),
            pltpu.VMEM((2, TOK, CH), BF16),
            pltpu.VMEM((LAYERS, TOK, RANK), F32),
            pltpu.VMEM((LAYERS, TOK, RANK), BF16),
            pltpu.VMEM((LAYERS, TOK, 128), F32),
            pltpu.VMEM((2, 4, 2 * RANK, TILE), BF16),
            pltpu.VMEM((LAYERS, 2, 2 * RANK, TILE), BF16),
            pltpu.VMEM((2, 4, 4, 32, TILE), BF16),
            pltpu.VMEM((2, 4, 4, 32, TILE), BF16),
            pltpu.VMEM((LAYERS, 3, 4, 32, TILE), BF16),
            pltpu.VMEM((LAYERS, 3, 4, 32, TILE), BF16),
            pltpu.VMEM((2, 4, 32, TILE), BF16),
            pltpu.VMEM((2, 4, 32, TILE), BF16),
            pltpu.VMEM((LAYERS, 3, 32, TILE), BF16),
            pltpu.VMEM((LAYERS, 3, 32, TILE), BF16),
            pltpu.VMEM((LAYERS, 32, TILE), BF16),
            pltpu.VMEM((LAYERS, 32, TILE), BF16),
            pltpu.VMEM((2, LAYERS, 32, TILE), BF16),
            dma((ZN - 1,)),
            dma((ZN - 1,)),
            dma,
            dma((2,)),
            dma((2, ZN - 1)),
            dma((2, ZN - 1)),
            dma((2, 3)),
            dma((2, LAYERS)),
            dma((2, 2)),
            dma((2, 2)),
            dma((5,)),
            dma((2, LAYERS, 2)),
            dma((2, LAYERS, 2)),
            dma((2, LAYERS)),
            dma((2, LAYERS)),
            dma((2, 2)),
            dma((LAYERS, 2)),
            dma((2, 2, 3)),
            dma((LAYERS, 2, 3)),
            dma((2, 2, 3)),
            dma((LAYERS, 2, 3)),
            dma((LAYERS, 2)),
            dma((2, LAYERS)),
        ],
        compiler_params=pltpu.CompilerParams(
            collective_id=0, has_side_effects=True, vmem_limit_bytes=60 * 1024 * 1024
        ),
        name="relay",
    )(inputs, adapter_down, adapter_up, value_weight, returns, targets)
    mine = part.astype(F32)
    return (mine[0].T[None], mine[1][None])


def solution(mesh):
    return jax.shard_map(
        shards,
        mesh=mesh,
        in_specs=(
            P(None, "dp", None),
            P(None, "dp"),
            P("pipe", None, None),
            P("pipe", None, None),
            P(),
            P(),
        ),
        out_specs=(P("pipe", "dp", None), P("pipe", None, "dp")),
        check_vma=False,
    )
```

```python
import functools

import jax
import jax.numpy as jnp
from jax import lax
from jax.experimental import pallas as pl
from jax.experimental.pallas import tpu as pltpu
from jax.sharding import PartitionSpec as P

LAYERS = 8
ZN = 4
TOK = 128
OWN = TOK // ZN
CH = 2048
RANK = 256
FEAT = 8192
TILE = 512
F32 = jnp.float32
BF16 = jnp.bfloat16
MESH = pl.DeviceIdType.MESH


def split3(row):
    hi = row.astype(BF16)
    rest = row - hi.astype(F32)
    mid = rest.astype(BF16)
    lo = (rest - mid.astype(F32)).astype(BF16)
    return [hi.astype(F32), mid.astype(F32), lo.astype(F32)]


def pack_rows(rows):
    parts = []
    for row in rows:
        parts += split3(row)
    at = lax.broadcasted_iota(jnp.int32, (16, 128), 0)
    tile = jnp.zeros((16, 128), F32)
    for i, part in enumerate(parts):
        tile = jnp.where(at == i, jnp.broadcast_to(part, (16, 128)), tile)
    return tile.astype(BF16)


def column(row):
    return jnp.transpose(jnp.broadcast_to(row, (TOK, 128)))


def row_sums(acc):
    return jnp.sum(jnp.transpose(acc), axis=0, keepdims=True)


def fold_lanes(tile):
    total = tile[:, 0:128]
    for i in range(1, tile.shape[1] // 128):
        total = total + tile[:, 128 * i : 128 * (i + 1)]
    return total


def wide(col, width):
    return jnp.concatenate([col] * (width // 128), axis=1)


def dot(a, b):
    return lax.dot_general(a, b, (((1,), (0,)), ((), ())), preferred_element_type=F32)


def dot_nt(a, b):
    return lax.dot_general(a, b, (((1,), (1,)), ((), ())), preferred_element_type=F32)


def dot_tn(a, b):
    return lax.dot_general(a, b, (((0,), (0,)), ((), ())), preferred_element_type=F32)


def kernel(
    x_hbm, wd_hbm, wu_hbm, vw_hbm, ret_hbm, targets_ref, down_ref, up_ref,
    vw_s, ret_s,
    xs, wd, wu, snd, rcv, mine, gx, pre_s, act_s, scale_s,
    gbuf, cbuf, dsum, usum, d1, u1, d2s, u2s, d2, u2, d3s, u3s, res,
    x_ssem, x_rsem, lsem, wsem, ssem, rsem,
    y_ssem, y_rsem, r_ssem, r_rsem, vsem, n_ssem, n_rsem, c_ssem, c_rsem,
    gc_ssem, gc_rsem, g1_ssem, g1_rsem, g2_ssem, g2_rsem, g3_ssem, g3_rsem,
):
    dp = lax.axis_index("dp")
    pipe = lax.axis_index("pipe")
    z = dp // 4
    c = lax.rem(dp, 2)
    xh = lax.rem(dp // 2, 2)
    rest = lax.rem(dp, 4)
    xl = pipe // 4
    y = lax.rem(pipe, 4)
    x = xh * 2 + xl
    zs = [lax.rem(z + i, ZN) for i in range(1, ZN)]
    peers = [(zz * 4 + rest, pipe) for zz in zs]
    core_peer = (dp + 1 - 2 * c, pipe)

    def x_dev(xx):
        return (z * 4 + (xx // 2) * 2 + c, lax.rem(xx, 2) * 4 + y)

    def y_dev(yy):
        return (dp, xl * 4 + yy)

    x_at = [lax.rem(x + i, 4) for i in range(1, 4)]
    y_at = [lax.rem(y + i, 4) for i in range(1, 4)]

    def remote(src, dst, send, recv, device):
        return pltpu.make_async_remote_copy(
            src_ref=src, dst_ref=dst, send_sem=send, recv_sem=recv,
            device_id=device, device_id_type=MESH,
        )

    feats = pl.ds(pl.multiple_of(z * CH, CH), CH)
    own_down = pltpu.make_async_copy(wd_hbm.at[0, feats, :], wd.at[pipe], wsem.at[0])
    own_up = pltpu.make_async_copy(wu_hbm.at[0, :, feats], wu.at[pipe], wsem.at[1])
    own_down.start()
    own_up.start()

    def piece(zz):
        return x_hbm.at[y, pl.ds(pl.multiple_of(xl * OWN, OWN), OWN), pl.ds(pl.multiple_of(zz * CH, CH), CH)]

    own_rows = pl.ds(pl.multiple_of(z * OWN, OWN), OWN)
    own = pltpu.make_async_copy(piece(z), xs.at[0, own_rows], lsem)
    own.start()
    small = pltpu.make_async_copy(vw_hbm.at[feats], vw_s.at[0], vsem.at[4])
    small.start()
    ret_copies = [
        pltpu.make_async_copy(ret_hbm.at[pl.ds(128 * i, 128)], ret_s.at[i], vsem.at[i]) for i in range(4)
    ]
    for copy in ret_copies:
        copy.start()

    barrier = pltpu.get_barrier_semaphore()
    greet = peers + [core_peer, x_dev(x_at[0]), x_dev(x_at[1]), x_dev(x_at[2])]
    greet += [(dp, lax.rem(pipe + i, LAYERS)) for i in range(1, LAYERS)]
    for device in greet:
        pl.semaphore_signal(barrier, inc=1, device_id=device, device_id_type=MESH)
    pl.semaphore_wait(barrier, len(greet))

    HALF = CH // 2
    QUART = CH // 4

    def y_copy(which, i, layer):
        at = pl.ds(pl.multiple_of(c * HALF, HALF), HALF)
        far = pl.ds(pl.multiple_of(z * CH + c * HALF, HALF), HALF)
        if which == 0:
            src, dst = wd_hbm.at[0, far, :], wd.at[layer, at, :]
        else:
            src, dst = wu_hbm.at[0, :, far], wu.at[layer, :, at]
        return remote(src, dst, y_ssem.at[which, i], y_rsem.at[which, layer], y_dev(y_at[i]))

    def quarter(which, layer, h):
        at = pl.ds(pl.multiple_of(c * HALF + h * QUART, QUART), QUART)
        return wd.at[layer, at, :] if which == 0 else wu.at[layer, :, at]

    def r_copy(which, layer, h):
        ref = quarter(which, layer, h)
        return remote(ref, ref, r_ssem.at[which, h], r_rsem.at[which, h], y_dev(y_at[2 * h]))

    def n_copy(which, layer, h):
        ref = quarter(which, layer, h)
        return remote(ref, ref, n_ssem.at[which, layer, h], n_rsem.at[which, layer, h], x_dev(x_at[2 * h]))

    def c_copy(which, layer):
        at = pl.ds(pl.multiple_of(c * HALF, HALF), HALF)
        ref = wd.at[layer, at, :] if which == 0 else wu.at[layer, :, at]
        return remote(ref, ref, c_ssem.at[which, layer], c_rsem.at[which, layer], core_peer)

    copies = []
    for i in range(ZN - 1):
        copy = remote(piece(zs[i]), xs.at[0, own_rows], x_ssem.at[i], x_rsem.at[i], peers[i])
        copy.start()
        copies.append(copy)
    for which in (0, 1):
        for i in (0, 2):
            y_copy(which, i, pipe).start()
        (own_down if which == 0 else own_up).wait()
        if which == 0:
            for h in (0, 1):
                n_copy(which, pipe, h).start()
        else:

            @pl.when(y < 2)
            def _():
                for h in (0, 1):
                    n_copy(1, pipe, h).start()

    def column_layer(i):
        return xl * 4 + y_at[i]

    def spread(which):
        for i, h in ((2, 0), (0, 1)):
            layer = column_layer(i)
            y_copy(which, 0, layer).wait_recv()
            r_copy(which, layer, h).start()
            c_copy(which, layer).start()
        for j in range(4):
            layer = xl * 4 + j

            @pl.when(y_at[1] == j)
            def _():
                for h in (0, 1):
                    r_copy(which, layer, h).wait_recv()
                    n_copy(which, layer, h).start()
                c_copy(which, layer).start()

            later = (y == j) & (j >= 2) if which == 1 else False
            @pl.when((y != j) & (y_at[1] != j) | later)
            def _():
                for h in (0, 1):
                    n_copy(which, layer, h).start()

    def pass_on(which, layer):
        @pl.when(layer // 4 != xl)
        def _():
            n_copy(which, layer, 0).wait_recv()
            n_copy(which, layer, 1).wait_recv()
            c_copy(which, layer).start()

    def wait_weights(which, layer):
        @pl.when(layer != pipe)
        def _():
            c_copy(which, layer).wait_recv()

    def sent_weights(which, layer):
        @pl.when(layer // 4 == xl)
        def _():
            n_copy(which, layer, 0).wait_send()
            n_copy(which, layer, 1).wait_send()

        @pl.when(layer != pipe)
        def _():
            c_copy(which, layer).wait_send()

    def exchange(slot, rows):
        return [
            remote(
                snd.at[slot, pl.ds(0, rows)], rcv.at[slot, i, pl.ds(0, rows)],
                ssem.at[slot, i], rsem.at[slot, i], peers[i],
            )
            for i in range(ZN - 1)
        ]

    def begin(copies):
        for copy in copies:
            copy.start()

    def begin_exchange(slot, rows):
        first, far, last = exchange(slot, rows)
        begin([far, first, last])

    def finish(copies):
        for copy in copies:
            copy.wait()

    def cols(t):
        return slice(t * TILE, (t + 1) * TILE)

    def send_product(slot, product, square):
        mine[...] = product
        snd[slot, 16 : 16 + TOK] = product.astype(BF16)
        row = row_sums(square)
        snd[slot, 0:16, 0:128] = pack_rows([row])
        return row

    def row_total(slot, first, own_row):
        total = own_row
        for i in range(ZN - 1):
            part = rcv[slot, i, 0:16, 0:128].astype(F32)[first : first + 3]
            total = total + jnp.sum(part, axis=0, keepdims=True)
        return total

    snd[...] = jnp.zeros_like(snd)
    own.wait()
    finish(copies)
    wanted = targets_ref[pl.ds(y, 1), :].astype(F32)
    wanted = column(jnp.concatenate([wanted, jnp.zeros_like(wanted)], axis=1))
    lane = lax.broadcasted_iota(jnp.int32, (TOK, 128), 1)
    small.wait()
    for copy in ret_copies:
        copy.wait()
    found = jnp.zeros((TOK, 128), F32)
    for i in range(4):
        agent = (lane + 128 * i).astype(F32)
        found += jnp.where(wanted == agent, jnp.broadcast_to(ret_s[i : i + 1, :], (TOK, 128)), 0.0)
    target_tile = pltpu.roll(
        jnp.broadcast_to(row_sums(found), (8, 128)), lax.rem(z * OWN + 128 - xl * OWN, 128), axis=1
    )
    target_tile = jnp.where((lane[:8] >= z * OWN) & (lane[:8] < z * OWN + OWN), target_tile, 0.0)
    target_row = target_tile[0:1]
    spread(0)
    pass_on(0, 0)
    wait_weights(0, 0)
    product = jnp.zeros((TOK, RANK), F32)
    square = jnp.zeros((TOK, 128), F32)
    for t in range(CH // TILE):
        tile = xs[0, :, cols(t)]
        wide_tile = tile.astype(F32)
        square += fold_lanes(wide_tile * wide_tile)
        product += dot(tile, wd[0, cols(t), :])
    own_row = send_product(0, product, square)

    def forward(layer, own_row):
        slot = lax.rem(layer, 2)
        begin_exchange(slot, 16 + TOK)

        @pl.when(layer == 0)
        def _():
            pass_on(0, 1)
            spread(1)
            pass_on(1, 0)

        @pl.when(layer < LAYERS - 1)
        def _():
            pass_on(1, layer + 1)

        @pl.when(layer < LAYERS - 2)
        def _():
            pass_on(0, layer + 2)

        finish(exchange(slot, 16 + TOK))
        total = mine[...]
        for i in range(ZN - 1):
            total = total + rcv[slot, i, 16 : 16 + TOK].astype(F32)
        ssq = row_total(slot, 0, own_row)
        scale = column(lax.rsqrt(ssq * (1.0 / FEAT) + 1e-05))
        pre = total * wide(scale, RANK)
        act = (pre / (1.0 + jnp.exp(-pre))).astype(BF16)
        scale_s[layer] = scale
        pre_s[layer] = pre
        act_s[layer] = act
        after = jnp.minimum(layer + 1, LAYERS - 1)
        wait_weights(1, layer)

        @pl.when(layer < LAYERS - 1)
        def _():
            wait_weights(0, layer + 1)

        product = jnp.zeros((TOK, RANK), F32)
        square = jnp.zeros((TOK, 128), F32)
        for t in range(CH // TILE):
            tile = (xs[layer, :, cols(t)].astype(F32) + dot(act, wu[layer, :, cols(t)])).astype(BF16)
            xs[layer + 1, :, cols(t)] = tile
            wide_tile = tile.astype(F32)
            square += fold_lanes(wide_tile * wide_tile)
            product += dot(tile, wd[after, cols(t), :])
        return send_product(1 - slot, product, square)

    own_row = lax.fori_loop(0, LAYERS, forward, own_row)

    value_acc = jnp.zeros((TOK, 128), F32)
    for t in range(CH // TILE):
        weight = vw_s[0:1, cols(t)]
        value_acc += fold_lanes(xs[LAYERS, :, cols(t)].astype(F32) * weight)
    value_row = row_sums(value_acc)
    snd[0, 0:16, 0:128] = pack_rows([own_row, value_row, target_row])
    begin_exchange(0, 16)
    for which in (0, 1):
        for i in (0, 2):
            y_copy(which, i, pipe).wait_send()
        for h in (0, 1):
            r_copy(which, pipe, h).wait_send()
        for layer in range(LAYERS):
            sent_weights(which, layer)
    finish(exchange(0, 16))
    ssq = row_total(0, 0, own_row)
    raw = row_total(0, 3, value_row)
    target = row_total(0, 6, target_row)
    scale = lax.rsqrt(ssq * (1.0 / FEAT) + 1e-05)
    value = scale * raw
    resid = value - target
    on_weight = column(scale * resid)
    on_x = column(-scale * scale * resid * value * (1.0 / FEAT))
    product = jnp.zeros((TOK, RANK), F32)
    for t in range(CH // TILE):
        weight = vw_s[0:1, cols(t)]
        tile = (
            wide(on_weight, TILE) * weight + wide(on_x, TILE) * xs[LAYERS, :, cols(t)].astype(F32)
        ).astype(BF16)
        gx[0, :, cols(t)] = tile
        product += dot_nt(tile, wu[LAYERS - 1, :, cols(t)])
    mine[...] = product
    snd[1, 16 : 16 + TOK] = product.astype(BF16)
    begin_exchange(1, 16 + TOK)

    def core_copy(layer, half):
        slot = lax.rem(layer, 2)
        return remote(
            gbuf.at[slot, 2 * half + 1 - c], cbuf.at[layer, half],
            gc_ssem.at[slot, half], gc_rsem.at[layer, half], core_peer,
        )

    def first_copies(layer):
        slot = lax.rem(layer, 4)
        found = []
        for i in range(3):
            found.append(remote(
                dsum.at[slot, x_at[i]], d1.at[layer, i],
                g1_ssem.at[slot, 0, i], g1_rsem.at[layer, 0, i], x_dev(x_at[i]),
            ))
            found.append(remote(
                usum.at[slot, y_at[i]], u1.at[layer, i],
                g1_ssem.at[slot, 1, i], g1_rsem.at[layer, 1, i], y_dev(y_at[i]),
            ))
        return found

    def second_copies(layer):
        slot = lax.rem(layer, 2)
        found = []
        for i in range(3):
            found.append(remote(
                d2s.at[slot, y_at[i]], d2.at[layer, i],
                g2_ssem.at[slot, 0, i], g2_rsem.at[layer, 0, i], y_dev(y_at[i]),
            ))
            found.append(remote(
                u2s.at[slot, x_at[i]], u2.at[layer, i],
                g2_ssem.at[slot, 1, i], g2_rsem.at[layer, 1, i], x_dev(x_at[i]),
            ))
        return found

    def last_copies(layer):
        return [
            remote(src.at[layer], res.at[which, pipe], g3_ssem.at[layer, which], g3_rsem.at[which, pipe], (dp, layer))
            for which, src in ((0, d3s), (1, u3s))
        ]

    def add_cores(layer):
        slot = lax.rem(layer, 2)
        for half in (0, 1):
            core_copy(layer, half).wait()
        deep = lax.rem(layer, 4)
        for half in (0, 1):
            for block in range(2):
                for part in range(4):
                    at = slice(block * 128 + part * 32, block * 128 + part * 32 + 32)
                    dsum[deep, 2 * half + block, part] = (
                        gbuf[slot, 2 * half + c, at].astype(F32) + cbuf[layer, half, at].astype(F32)
                    ).astype(BF16)
                    at = slice(RANK + at.start, RANK + at.stop)
                    usum[deep, part, 2 * half + block] = (
                        gbuf[slot, 2 * half + c, at].astype(F32) + cbuf[layer, half, at].astype(F32)
                    ).astype(BF16)
        begin(first_copies(layer))

    def add_first(layer):
        slot = lax.rem(layer, 2)
        finish(first_copies(layer))
        for part in range(4):
            for total, at, got, to in ((dsum, x, d1, d2s), (usum, y, u1, u2s)):
                value = total[lax.rem(layer, 4), at, part].astype(F32)
                for i in range(3):
                    value = value + got[layer, i, part].astype(F32)
                to[slot, part] = value.astype(BF16)
        begin(second_copies(layer))

    def add_second(layer):
        slot = lax.rem(layer, 2)
        finish(second_copies(layer))
        done = []
        for total, at, got in ((d2s, y, d2), (u2s, x, u2)):
            value = total[slot, at].astype(F32)
            for i in range(3):
                value = value + got[layer, i].astype(F32)
            done.append(value.astype(BF16))

        @pl.when(layer == pipe)
        def _():
            res[0, pipe] = done[0]
            res[1, pipe] = done[1]

        @pl.when(layer != pipe)
        def _():
            d3s[layer] = done[0]
            u3s[layer] = done[1]
            begin(last_copies(layer))

    def sums(step):
        @pl.when((step >= 1) & (step < LAYERS + 1))
        def _():
            add_cores(LAYERS - step)

        @pl.when((step >= 3) & (step < LAYERS + 3))
        def _():
            add_first(LAYERS + 2 - step)

        @pl.when(step >= 4)
        def _():
            add_second(LAYERS + 3 - step)

    def backward(step, carry):
        layer = LAYERS - 1 - step
        slot = lax.rem(step + 1, 2)
        now = lax.rem(step, 2)
        finish(exchange(slot, 16 + TOK))
        total = mine[...]
        for i in range(ZN - 1):
            total = total + rcv[slot, i, 16 : 16 + TOK].astype(F32)
        pre = pre_s[layer]
        scale = scale_s[layer]
        sigma = 1.0 / (1.0 + jnp.exp(-pre))
        grad_pre = (total * sigma * (1.0 + pre * (1.0 - sigma))).astype(BF16)
        grad_f = grad_pre.astype(F32)
        inner = jnp.sum(grad_f * pre, axis=1, keepdims=True) * (1.0 / FEAT)
        scaled = (grad_f * wide(scale, RANK)).astype(BF16)

        @pl.when(layer > 0)
        def _():
            on_x = wide(scale * scale * inner, TILE)
            on_q = wide(scale, TILE)
            product = jnp.zeros((TOK, RANK), F32)
            for t in range(CH // TILE):
                q = dot_nt(grad_pre, wd[layer, cols(t), :])
                tile = (
                    gx[now, :, cols(t)].astype(F32) + on_q * q - on_x * xs[layer, :, cols(t)].astype(F32)
                ).astype(BF16)
                gx[1 - now, :, cols(t)] = tile
                product += dot_nt(tile, wu[layer - 1, :, cols(t)])
            mine[...] = product
            snd[1 - slot, 16 : 16 + TOK] = product.astype(BF16)
            begin_exchange(1 - slot, 16 + TOK)

        act = act_s[layer]
        turn = lax.rem(layer, 2)
        for t in range(CH // TILE):
            gbuf[turn, t, 0:RANK] = dot_tn(scaled, xs[layer, :, cols(t)]).astype(BF16)
            gbuf[turn, t, RANK : 2 * RANK] = dot_tn(act, gx[now, :, cols(t)]).astype(BF16)
        for half in (0, 1):
            core_copy(layer, half).start()
        sums(step)
        return carry

    lax.fori_loop(0, LAYERS, backward, 0)

    def rest_of_sums(step, carry):
        sums(step)
        return carry

    lax.fori_loop(LAYERS, LAYERS + 4, rest_of_sums, 0)

    def finish_last(layer, carry):
        @pl.when(layer != pipe)
        def _():
            for copy in last_copies(layer):
                copy.wait_send()
            for which in (0, 1):
                remote(
                    d3s.at[layer], res.at[which, layer],
                    g3_ssem.at[layer, which], g3_rsem.at[which, layer], (dp, layer),
                ).wait_recv()
        return carry

    lax.fori_loop(0, LAYERS, finish_last, 0)
    down = jnp.concatenate([res[0, part].astype(F32) for part in range(LAYERS)], axis=0)
    down_ref[...] = jnp.transpose(down).astype(BF16)
    for part in range(LAYERS):
        up_ref[part * 32 : part * 32 + 32] = res[1, part]


def shards(inputs, targets, adapter_down, adapter_up, value_weight, returns):
    any_spec = pl.BlockSpec(memory_space=pl.ANY)
    vmem = pl.BlockSpec(memory_space=pltpu.VMEM)
    dma = pltpu.SemaphoreType.DMA
    down, up = pl.pallas_call(
        kernel,
        out_shape=(
            jax.ShapeDtypeStruct((TILE, RANK), BF16),
            jax.ShapeDtypeStruct((RANK, TILE), BF16),
        ),
        in_specs=[any_spec, any_spec, any_spec, any_spec, any_spec, vmem],
        out_specs=(vmem, vmem),
        scratch_shapes=[
            pltpu.VMEM((8, CH), F32),
            pltpu.VMEM((8, 128), F32),
            pltpu.VMEM((LAYERS + 1, TOK, CH), BF16),
            pltpu.VMEM((LAYERS, CH, RANK), BF16),
            pltpu.VMEM((LAYERS, RANK, CH), BF16),
            pltpu.VMEM((2, 16 + TOK, RANK), BF16),
            pltpu.VMEM((2, ZN - 1, 16 + TOK, RANK), BF16),
            pltpu.VMEM((TOK, RANK), F32),
            pltpu.VMEM((2, TOK, CH), BF16),
            pltpu.VMEM((LAYERS, TOK, RANK), F32),
            pltpu.VMEM((LAYERS, TOK, RANK), BF16),
            pltpu.VMEM((LAYERS, TOK, 128), F32),
            pltpu.VMEM((2, 4, 2 * RANK, TILE), BF16),
            pltpu.VMEM((LAYERS, 2, 2 * RANK, TILE), BF16),
            pltpu.VMEM((4, 4, 4, 32, TILE), BF16),
            pltpu.VMEM((4, 4, 4, 32, TILE), BF16),
            pltpu.VMEM((LAYERS, 3, 4, 32, TILE), BF16),
            pltpu.VMEM((LAYERS, 3, 4, 32, TILE), BF16),
            pltpu.VMEM((2, 4, 32, TILE), BF16),
            pltpu.VMEM((2, 4, 32, TILE), BF16),
            pltpu.VMEM((LAYERS, 3, 32, TILE), BF16),
            pltpu.VMEM((LAYERS, 3, 32, TILE), BF16),
            pltpu.VMEM((LAYERS, 32, TILE), BF16),
            pltpu.VMEM((LAYERS, 32, TILE), BF16),
            pltpu.VMEM((2, LAYERS, 32, TILE), BF16),
            dma((ZN - 1,)),
            dma((ZN - 1,)),
            dma,
            dma((2,)),
            dma((2, ZN - 1)),
            dma((2, ZN - 1)),
            dma((2, 3)),
            dma((2, LAYERS)),
            dma((2, 2)),
            dma((2, 2)),
            dma((5,)),
            dma((2, LAYERS, 2)),
            dma((2, LAYERS, 2)),
            dma((2, LAYERS)),
            dma((2, LAYERS)),
            dma((2, 2)),
            dma((LAYERS, 2)),
            dma((4, 2, 3)),
            dma((LAYERS, 2, 3)),
            dma((2, 2, 3)),
            dma((LAYERS, 2, 3)),
            dma((LAYERS, 2)),
            dma((2, LAYERS)),
        ],
        compiler_params=pltpu.CompilerParams(
            collective_id=0, has_side_effects=True, vmem_limit_bytes=60 * 1024 * 1024
        ),
        name="relay",
    )(inputs, adapter_down, adapter_up, value_weight, returns, targets)
    return (down.astype(F32)[None], up.astype(F32)[None])


def solution(mesh):
    return jax.shard_map(
        shards,
        mesh=mesh,
        in_specs=(
            P(None, "dp", None),
            P(None, "dp"),
            P("pipe", None, None),
            P("pipe", None, None),
            P(),
            P(),
        ),
        out_specs=(P("pipe", "dp", None), P("pipe", None, "dp")),
        check_vma=False,
    )
```

```python
import functools

import jax
import jax.numpy as jnp
from jax import lax
from jax.experimental import pallas as pl
from jax.experimental.pallas import tpu as pltpu
from jax.sharding import PartitionSpec as P

LAYERS = 8
ZN = 4
TOK = 128
OWN = TOK // ZN
CH = 2048
RANK = 256
FEAT = 8192
TILE = 512
F32 = jnp.float32
BF16 = jnp.bfloat16
MESH = pl.DeviceIdType.MESH


def split3(row):
    hi = row.astype(BF16)
    rest = row - hi.astype(F32)
    mid = rest.astype(BF16)
    lo = (rest - mid.astype(F32)).astype(BF16)
    return [hi.astype(F32), mid.astype(F32), lo.astype(F32)]


def pack_rows(rows):
    parts = []
    for row in rows:
        parts += split3(row)
    at = lax.broadcasted_iota(jnp.int32, (16, 128), 0)
    tile = jnp.zeros((16, 128), F32)
    for i, part in enumerate(parts):
        tile = jnp.where(at == i, jnp.broadcast_to(part, (16, 128)), tile)
    return tile.astype(BF16)


def column(row):
    return jnp.transpose(jnp.broadcast_to(row, (TOK, 128)))


def row_sums(acc):
    return jnp.sum(jnp.transpose(acc), axis=0, keepdims=True)


def fold_lanes(tile):
    total = tile[:, 0:128]
    for i in range(1, tile.shape[1] // 128):
        total = total + tile[:, 128 * i : 128 * (i + 1)]
    return total


def wide(col, width):
    return jnp.concatenate([col] * (width // 128), axis=1)


def dot(a, b):
    return lax.dot_general(a, b, (((1,), (0,)), ((), ())), preferred_element_type=F32)


def dot_nt(a, b):
    return lax.dot_general(a, b, (((1,), (1,)), ((), ())), preferred_element_type=F32)


def dot_tn(a, b):
    return lax.dot_general(a, b, (((0,), (0,)), ((), ())), preferred_element_type=F32)


def kernel(
    x_hbm, wd_hbm, wu_hbm, vw_hbm, ret_hbm, targets_ref, down_ref, up_ref,
    vw_s, ret_s,
    xs, wd, wu, snd, rcv, mine, gx, pre_s, act_s, scale_s,
    gbuf, cbuf, dsum, usum, m1, d1, u1, d2s, u2s, d2, u2, d3s, u3s, res,
    x_ssem, x_rsem, lsem, wsem, ssem, rsem,
    y_ssem, y_rsem, r_ssem, r_rsem, vsem, n_ssem, n_rsem, c_ssem, c_rsem,
    gc_ssem, gc_rsem, gm_ssem, gm_rsem, g1_ssem, g1_rsem, g2_ssem, g2_rsem, g3_ssem, g3_rsem,
):
    dp = lax.axis_index("dp")
    pipe = lax.axis_index("pipe")
    z = dp // 4
    c = lax.rem(dp, 2)
    xh = lax.rem(dp // 2, 2)
    rest = lax.rem(dp, 4)
    xl = pipe // 4
    y = lax.rem(pipe, 4)
    x = xh * 2 + xl
    zs = [lax.rem(z + i, ZN) for i in range(1, ZN)]
    peers = [(zz * 4 + rest, pipe) for zz in zs]
    core_peer = (dp + 1 - 2 * c, pipe)

    def x_dev(xx):
        return (z * 4 + (xx // 2) * 2 + c, lax.rem(xx, 2) * 4 + y)

    def y_dev(yy):
        return (dp, xl * 4 + yy)

    x_at = [lax.rem(x + i, 4) for i in range(1, 4)]
    y_at = [lax.rem(y + i, 4) for i in range(1, 4)]

    def remote(src, dst, send, recv, device):
        return pltpu.make_async_remote_copy(
            src_ref=src, dst_ref=dst, send_sem=send, recv_sem=recv,
            device_id=device, device_id_type=MESH,
        )

    feats = pl.ds(pl.multiple_of(z * CH, CH), CH)
    own_down = pltpu.make_async_copy(wd_hbm.at[0, feats, :], wd.at[pipe], wsem.at[0])
    own_up = pltpu.make_async_copy(wu_hbm.at[0, :, feats], wu.at[pipe], wsem.at[1])
    own_down.start()
    own_up.start()

    def piece(zz):
        return x_hbm.at[y, pl.ds(pl.multiple_of(xl * OWN, OWN), OWN), pl.ds(pl.multiple_of(zz * CH, CH), CH)]

    own_rows = pl.ds(pl.multiple_of(z * OWN, OWN), OWN)
    own = pltpu.make_async_copy(piece(z), xs.at[0, own_rows], lsem)
    own.start()
    small = pltpu.make_async_copy(vw_hbm.at[feats], vw_s.at[0], vsem.at[4])
    small.start()
    ret_copies = [
        pltpu.make_async_copy(ret_hbm.at[pl.ds(128 * i, 128)], ret_s.at[i], vsem.at[i]) for i in range(4)
    ]
    for copy in ret_copies:
        copy.start()

    barrier = pltpu.get_barrier_semaphore()
    greet = peers + [core_peer, x_dev(x_at[0]), x_dev(x_at[1]), x_dev(x_at[2])]
    greet += [(dp, lax.rem(pipe + i, LAYERS)) for i in range(1, LAYERS)]
    for device in greet:
        pl.semaphore_signal(barrier, inc=1, device_id=device, device_id_type=MESH)
    pl.semaphore_wait(barrier, len(greet))

    HALF = CH // 2
    QUART = CH // 4

    def y_copy(which, i, layer):
        at = pl.ds(pl.multiple_of(c * HALF, HALF), HALF)
        far = pl.ds(pl.multiple_of(z * CH + c * HALF, HALF), HALF)
        if which == 0:
            src, dst = wd_hbm.at[0, far, :], wd.at[layer, at, :]
        else:
            src, dst = wu_hbm.at[0, :, far], wu.at[layer, :, at]
        return remote(src, dst, y_ssem.at[which, i], y_rsem.at[which, layer], y_dev(y_at[i]))

    def quarter(which, layer, h):
        at = pl.ds(pl.multiple_of(c * HALF + h * QUART, QUART), QUART)
        return wd.at[layer, at, :] if which == 0 else wu.at[layer, :, at]

    def r_copy(which, layer, h):
        ref = quarter(which, layer, h)
        return remote(ref, ref, r_ssem.at[which, h], r_rsem.at[which, h], y_dev(y_at[2 * h]))

    def n_copy(which, layer, h):
        ref = quarter(which, layer, h)
        return remote(ref, ref, n_ssem.at[which, layer, h], n_rsem.at[which, layer, h], x_dev(x_at[2 * h]))

    def c_copy(which, layer):
        at = pl.ds(pl.multiple_of(c * HALF, HALF), HALF)
        ref = wd.at[layer, at, :] if which == 0 else wu.at[layer, :, at]
        return remote(ref, ref, c_ssem.at[which, layer], c_rsem.at[which, layer], core_peer)

    copies = []
    for i in range(ZN - 1):
        copy = remote(piece(zs[i]), xs.at[0, own_rows], x_ssem.at[i], x_rsem.at[i], peers[i])
        copy.start()
        copies.append(copy)
    def start_own(which):
        for i in (0, 2):
            y_copy(which, i, pipe).start()
        (own_down if which == 0 else own_up).wait()
        if which == 0:
            for h in (0, 1):
                n_copy(which, pipe, h).start()
        else:

            @pl.when(y < 2)
            def _():
                for h in (0, 1):
                    n_copy(1, pipe, h).start()

    start_own(0)

    def column_layer(i):
        return xl * 4 + y_at[i]

    def spread(which):
        for i, h in ((2, 0), (0, 1)):
            layer = column_layer(i)
            y_copy(which, 0, layer).wait_recv()
            r_copy(which, layer, h).start()
            c_copy(which, layer).start()
        for j in range(4):
            layer = xl * 4 + j

            @pl.when(y_at[1] == j)
            def _():
                for h in (0, 1):
                    r_copy(which, layer, h).wait_recv()
                    n_copy(which, layer, h).start()
                c_copy(which, layer).start()

            later = (y == j) & (j >= 2) if which == 1 else False
            @pl.when((y != j) & (y_at[1] != j) | later)
            def _():
                for h in (0, 1):
                    n_copy(which, layer, h).start()

    def pass_on(which, layer):
        @pl.when(layer // 4 != xl)
        def _():
            n_copy(which, layer, 0).wait_recv()
            n_copy(which, layer, 1).wait_recv()
            c_copy(which, layer).start()

    def wait_weights(which, layer):
        @pl.when(layer != pipe)
        def _():
            c_copy(which, layer).wait_recv()

    def sent_weights(which, layer):
        @pl.when(layer // 4 == xl)
        def _():
            n_copy(which, layer, 0).wait_send()
            n_copy(which, layer, 1).wait_send()

        @pl.when(layer != pipe)
        def _():
            c_copy(which, layer).wait_send()

    def exchange(slot, rows):
        return [
            remote(
                snd.at[slot, pl.ds(0, rows)], rcv.at[slot, i, pl.ds(0, rows)],
                ssem.at[slot, i], rsem.at[slot, i], peers[i],
            )
            for i in range(ZN - 1)
        ]

    def begin(copies):
        for copy in copies:
            copy.start()

    def begin_exchange(slot, rows):
        first, far, last = exchange(slot, rows)
        begin([far, first, last])

    def finish(copies):
        for copy in copies:
            copy.wait()

    def cols(t):
        return slice(t * TILE, (t + 1) * TILE)

    def send_product(slot, product, square):
        mine[...] = product
        snd[slot, 16 : 16 + TOK] = product.astype(BF16)
        row = row_sums(square)
        snd[slot, 0:16, 0:128] = pack_rows([row])
        return row

    def row_total(slot, first, own_row):
        total = own_row
        for i in range(ZN - 1):
            part = rcv[slot, i, 0:16, 0:128].astype(F32)[first : first + 3]
            total = total + jnp.sum(part, axis=0, keepdims=True)
        return total

    snd[...] = jnp.zeros_like(snd)
    own.wait()
    finish(copies)
    wanted = targets_ref[pl.ds(y, 1), :].astype(F32)
    wanted = column(jnp.concatenate([wanted, jnp.zeros_like(wanted)], axis=1))
    lane = lax.broadcasted_iota(jnp.int32, (TOK, 128), 1)
    small.wait()
    for copy in ret_copies:
        copy.wait()
    found = jnp.zeros((TOK, 128), F32)
    for i in range(4):
        agent = (lane + 128 * i).astype(F32)
        found += jnp.where(wanted == agent, jnp.broadcast_to(ret_s[i : i + 1, :], (TOK, 128)), 0.0)
    target_tile = pltpu.roll(
        jnp.broadcast_to(row_sums(found), (8, 128)), lax.rem(z * OWN + 128 - xl * OWN, 128), axis=1
    )
    target_tile = jnp.where((lane[:8] >= z * OWN) & (lane[:8] < z * OWN + OWN), target_tile, 0.0)
    target_row = target_tile[0:1]
    spread(0)
    start_own(1)
    pass_on(0, 0)
    wait_weights(0, 0)
    product = jnp.zeros((TOK, RANK), F32)
    square = jnp.zeros((TOK, 128), F32)
    for t in range(CH // TILE):
        tile = xs[0, :, cols(t)]
        wide_tile = tile.astype(F32)
        square += fold_lanes(wide_tile * wide_tile)
        product += dot(tile, wd[0, cols(t), :])
    own_row = send_product(0, product, square)

    def forward(layer, own_row):
        slot = lax.rem(layer, 2)
        begin_exchange(slot, 16 + TOK)

        @pl.when(layer == 0)
        def _():
            pass_on(0, 1)
            spread(1)
            pass_on(1, 0)

        @pl.when(layer < LAYERS - 1)
        def _():
            pass_on(1, layer + 1)

        @pl.when(layer < LAYERS - 2)
        def _():
            pass_on(0, layer + 2)

        finish(exchange(slot, 16 + TOK))
        total = mine[...]
        for i in range(ZN - 1):
            total = total + rcv[slot, i, 16 : 16 + TOK].astype(F32)
        ssq = row_total(slot, 0, own_row)
        scale = column(lax.rsqrt(ssq * (1.0 / FEAT) + 1e-05))
        pre = total * wide(scale, RANK)
        act = (pre / (1.0 + jnp.exp(-pre))).astype(BF16)
        scale_s[layer] = scale
        pre_s[layer] = pre
        act_s[layer] = act
        after = jnp.minimum(layer + 1, LAYERS - 1)
        wait_weights(1, layer)

        @pl.when(layer < LAYERS - 1)
        def _():
            wait_weights(0, layer + 1)

        product = jnp.zeros((TOK, RANK), F32)
        square = jnp.zeros((TOK, 128), F32)
        for t in range(CH // TILE):
            tile = (xs[layer, :, cols(t)].astype(F32) + dot(act, wu[layer, :, cols(t)])).astype(BF16)
            xs[layer + 1, :, cols(t)] = tile
            wide_tile = tile.astype(F32)
            square += fold_lanes(wide_tile * wide_tile)
            product += dot(tile, wd[after, cols(t), :])
        return send_product(1 - slot, product, square)

    own_row = lax.fori_loop(0, LAYERS, forward, own_row)

    value_acc = jnp.zeros((TOK, 128), F32)
    for t in range(CH // TILE):
        weight = vw_s[0:1, cols(t)]
        value_acc += fold_lanes(xs[LAYERS, :, cols(t)].astype(F32) * weight)
    value_row = row_sums(value_acc)
    snd[0, 0:16, 0:128] = pack_rows([own_row, value_row, target_row])
    begin_exchange(0, 16)
    for which in (0, 1):
        for i in (0, 2):
            y_copy(which, i, pipe).wait_send()
        for h in (0, 1):
            r_copy(which, pipe, h).wait_send()
        for layer in range(LAYERS):
            sent_weights(which, layer)
    finish(exchange(0, 16))
    ssq = row_total(0, 0, own_row)
    raw = row_total(0, 3, value_row)
    target = row_total(0, 6, target_row)
    scale = lax.rsqrt(ssq * (1.0 / FEAT) + 1e-05)
    value = scale * raw
    resid = value - target
    on_weight = column(scale * resid)
    on_x = column(-scale * scale * resid * value * (1.0 / FEAT))
    product = jnp.zeros((TOK, RANK), F32)
    for t in range(CH // TILE):
        weight = vw_s[0:1, cols(t)]
        tile = (
            wide(on_weight, TILE) * weight + wide(on_x, TILE) * xs[LAYERS, :, cols(t)].astype(F32)
        ).astype(BF16)
        gx[0, :, cols(t)] = tile
        product += dot_nt(tile, wu[LAYERS - 1, :, cols(t)])
    mine[...] = product
    snd[1, 16 : 16 + TOK] = product.astype(BF16)
    begin_exchange(1, 16 + TOK)

    def core_copy(layer, half):
        slot = lax.rem(layer, 2)
        return remote(
            gbuf.at[slot, 2 * half + 1 - c], cbuf.at[layer, half],
            gc_ssem.at[slot, half], gc_rsem.at[layer, half], core_peer,
        )

    def middle_copies(layer):
        deep = lax.rem(layer, 4)
        found = []
        for k, i in ((0, 0), (1, 2)):
            found.append(remote(
                dsum.at[deep, x_at[1], pl.ds(2 * k, 2)], m1.at[0, layer, k],
                gm_ssem.at[deep, 0, k], gm_rsem.at[layer, 0, k], x_dev(x_at[i]),
            ))
            found.append(remote(
                usum.at[deep, y_at[1], pl.ds(2 * k, 2)], m1.at[1, layer, k],
                gm_ssem.at[deep, 1, k], gm_rsem.at[layer, 1, k], y_dev(y_at[i]),
            ))
        return found

    def first_copies(layer):
        deep = lax.rem(layer, 4)
        found = []
        for k, i in ((0, 0), (1, 2)):
            found.append(remote(
                dsum.at[deep, x_at[i]], d1.at[layer, k],
                g1_ssem.at[deep, 0, k], g1_rsem.at[layer, 0, k], x_dev(x_at[i]),
            ))
            found.append(remote(
                usum.at[deep, y_at[i]], u1.at[layer, k],
                g1_ssem.at[deep, 1, k], g1_rsem.at[layer, 1, k], y_dev(y_at[i]),
            ))
        return found

    def second_copies(layer):
        slot = lax.rem(layer, 2)
        found = []
        for i in range(3):
            found.append(remote(
                d2s.at[slot, y_at[i]], d2.at[layer, i],
                g2_ssem.at[slot, 0, i], g2_rsem.at[layer, 0, i], y_dev(y_at[i]),
            ))
            found.append(remote(
                u2s.at[slot, x_at[i]], u2.at[layer, i],
                g2_ssem.at[slot, 1, i], g2_rsem.at[layer, 1, i], x_dev(x_at[i]),
            ))
        return found

    def last_copies(layer):
        return [
            remote(src.at[layer], res.at[which, pipe], g3_ssem.at[layer, which], g3_rsem.at[which, pipe], (dp, layer))
            for which, src in ((0, d3s), (1, u3s))
        ]

    def add_cores(layer):
        slot = lax.rem(layer, 2)
        for half in (0, 1):
            core_copy(layer, half).wait()
        deep = lax.rem(layer, 4)
        for half in (0, 1):
            for block in range(2):
                for part in range(4):
                    at = slice(block * 128 + part * 32, block * 128 + part * 32 + 32)
                    dsum[deep, 2 * half + block, part] = (
                        gbuf[slot, 2 * half + c, at].astype(F32) + cbuf[layer, half, at].astype(F32)
                    ).astype(BF16)
                    at = slice(RANK + at.start, RANK + at.stop)
                    usum[deep, part, 2 * half + block] = (
                        gbuf[slot, 2 * half + c, at].astype(F32) + cbuf[layer, half, at].astype(F32)
                    ).astype(BF16)
        begin(middle_copies(layer))

    def add_middle(layer):
        deep = lax.rem(layer, 4)
        finish(middle_copies(layer))
        for k, i in ((0, 0), (1, 2)):
            for part in range(2):
                for which, total, at in ((0, dsum, x_at[i]), (1, usum, y_at[i])):
                    total[deep, at, 2 * k + part] = (
                        total[deep, at, 2 * k + part].astype(F32) + m1[which, layer, k, part].astype(F32)
                    ).astype(BF16)
        begin(first_copies(layer))

    def add_first(layer):
        slot = lax.rem(layer, 2)
        finish(first_copies(layer))
        for part in range(4):
            for total, at, got, to in ((dsum, x, d1, d2s), (usum, y, u1, u2s)):
                value = total[lax.rem(layer, 4), at, part].astype(F32)
                for i in range(2):
                    value = value + got[layer, i, part].astype(F32)
                to[slot, part] = value.astype(BF16)
        begin(second_copies(layer))

    def add_second(layer):
        slot = lax.rem(layer, 2)
        finish(second_copies(layer))
        done = []
        for total, at, got in ((d2s, y, d2), (u2s, x, u2)):
            value = total[slot, at].astype(F32)
            for i in range(3):
                value = value + got[layer, i].astype(F32)
            done.append(value.astype(BF16))

        @pl.when(layer == pipe)
        def _():
            res[0, pipe] = done[0]
            res[1, pipe] = done[1]

        @pl.when(layer != pipe)
        def _():
            d3s[layer] = done[0]
            u3s[layer] = done[1]
            begin(last_copies(layer))

    def sums(step):
        @pl.when((step >= 1) & (step < LAYERS + 1))
        def _():
            add_cores(LAYERS - step)

        @pl.when((step >= 2) & (step < LAYERS + 2))
        def _():
            add_middle(LAYERS + 1 - step)

        @pl.when((step >= 3) & (step < LAYERS + 3))
        def _():
            add_first(LAYERS + 2 - step)

        @pl.when(step >= 4)
        def _():
            add_second(LAYERS + 3 - step)

    def backward(step, carry):
        layer = LAYERS - 1 - step
        slot = lax.rem(step + 1, 2)
        now = lax.rem(step, 2)
        finish(exchange(slot, 16 + TOK))
        total = mine[...]
        for i in range(ZN - 1):
            total = total + rcv[slot, i, 16 : 16 + TOK].astype(F32)
        pre = pre_s[layer]
        scale = scale_s[layer]
        sigma = 1.0 / (1.0 + jnp.exp(-pre))
        grad_pre = (total * sigma * (1.0 + pre * (1.0 - sigma))).astype(BF16)
        grad_f = grad_pre.astype(F32)
        inner = jnp.sum(grad_f * pre, axis=1, keepdims=True) * (1.0 / FEAT)
        scaled = (grad_f * wide(scale, RANK)).astype(BF16)

        @pl.when(layer > 0)
        def _():
            on_x = wide(scale * scale * inner, TILE)
            on_q = wide(scale, TILE)
            product = jnp.zeros((TOK, RANK), F32)
            for t in range(CH // TILE):
                q = dot_nt(grad_pre, wd[layer, cols(t), :])
                tile = (
                    gx[now, :, cols(t)].astype(F32) + on_q * q - on_x * xs[layer, :, cols(t)].astype(F32)
                ).astype(BF16)
                gx[1 - now, :, cols(t)] = tile
                product += dot_nt(tile, wu[layer - 1, :, cols(t)])
            mine[...] = product
            snd[1 - slot, 16 : 16 + TOK] = product.astype(BF16)
            begin_exchange(1 - slot, 16 + TOK)

        act = act_s[layer]
        turn = lax.rem(layer, 2)
        for t in range(CH // TILE):
            gbuf[turn, t, 0:RANK] = dot_tn(scaled, xs[layer, :, cols(t)]).astype(BF16)
            gbuf[turn, t, RANK : 2 * RANK] = dot_tn(act, gx[now, :, cols(t)]).astype(BF16)
        for half in (0, 1):
            core_copy(layer, half).start()
        sums(step)
        return carry

    lax.fori_loop(0, LAYERS, backward, 0)

    def rest_of_sums(step, carry):
        sums(step)
        return carry

    lax.fori_loop(LAYERS, LAYERS + 4, rest_of_sums, 0)

    def finish_last(layer, carry):
        @pl.when(layer != pipe)
        def _():
            for copy in last_copies(layer):
                copy.wait_send()
            for which in (0, 1):
                remote(
                    d3s.at[layer], res.at[which, layer],
                    g3_ssem.at[layer, which], g3_rsem.at[which, layer], (dp, layer),
                ).wait_recv()
        return carry

    lax.fori_loop(0, LAYERS, finish_last, 0)
    down = jnp.concatenate([res[0, part].astype(F32) for part in range(LAYERS)], axis=0)
    down_ref[...] = jnp.transpose(down).astype(BF16)
    for part in range(LAYERS):
        up_ref[part * 32 : part * 32 + 32] = res[1, part]


def shards(inputs, targets, adapter_down, adapter_up, value_weight, returns):
    any_spec = pl.BlockSpec(memory_space=pl.ANY)
    vmem = pl.BlockSpec(memory_space=pltpu.VMEM)
    dma = pltpu.SemaphoreType.DMA
    down, up = pl.pallas_call(
        kernel,
        out_shape=(
            jax.ShapeDtypeStruct((TILE, RANK), BF16),
            jax.ShapeDtypeStruct((RANK, TILE), BF16),
        ),
        in_specs=[any_spec, any_spec, any_spec, any_spec, any_spec, vmem],
        out_specs=(vmem, vmem),
        scratch_shapes=[
            pltpu.VMEM((8, CH), F32),
            pltpu.VMEM((8, 128), F32),
            pltpu.VMEM((LAYERS + 1, TOK, CH), BF16),
            pltpu.VMEM((LAYERS, CH, RANK), BF16),
            pltpu.VMEM((LAYERS, RANK, CH), BF16),
            pltpu.VMEM((2, 16 + TOK, RANK), BF16),
            pltpu.VMEM((2, ZN - 1, 16 + TOK, RANK), BF16),
            pltpu.VMEM((TOK, RANK), F32),
            pltpu.VMEM((2, TOK, CH), BF16),
            pltpu.VMEM((LAYERS, TOK, RANK), F32),
            pltpu.VMEM((LAYERS, TOK, RANK), BF16),
            pltpu.VMEM((LAYERS, TOK, 128), F32),
            pltpu.VMEM((2, 4, 2 * RANK, TILE), BF16),
            pltpu.VMEM((LAYERS, 2, 2 * RANK, TILE), BF16),
            pltpu.VMEM((4, 4, 4, 32, TILE), BF16),
            pltpu.VMEM((4, 4, 4, 32, TILE), BF16),
            pltpu.VMEM((2, LAYERS, 2, 2, 32, TILE), BF16),
            pltpu.VMEM((LAYERS, 2, 4, 32, TILE), BF16),
            pltpu.VMEM((LAYERS, 2, 4, 32, TILE), BF16),
            pltpu.VMEM((2, 4, 32, TILE), BF16),
            pltpu.VMEM((2, 4, 32, TILE), BF16),
            pltpu.VMEM((LAYERS, 3, 32, TILE), BF16),
            pltpu.VMEM((LAYERS, 3, 32, TILE), BF16),
            pltpu.VMEM((LAYERS, 32, TILE), BF16),
            pltpu.VMEM((LAYERS, 32, TILE), BF16),
            pltpu.VMEM((2, LAYERS, 32, TILE), BF16),
            dma((ZN - 1,)),
            dma((ZN - 1,)),
            dma,
            dma((2,)),
            dma((2, ZN - 1)),
            dma((2, ZN - 1)),
            dma((2, 3)),
            dma((2, LAYERS)),
            dma((2, 2)),
            dma((2, 2)),
            dma((5,)),
            dma((2, LAYERS, 2)),
            dma((2, LAYERS, 2)),
            dma((2, LAYERS)),
            dma((2, LAYERS)),
            dma((2, 2)),
            dma((LAYERS, 2)),
            dma((4, 2, 2)),
            dma((LAYERS, 2, 2)),
            dma((4, 2, 2)),
            dma((LAYERS, 2, 2)),
            dma((2, 2, 3)),
            dma((LAYERS, 2, 3)),
            dma((LAYERS, 2)),
            dma((2, LAYERS)),
        ],
        compiler_params=pltpu.CompilerParams(
            collective_id=0, has_side_effects=True, vmem_limit_bytes=60 * 1024 * 1024
        ),
        name="relay",
    )(inputs, adapter_down, adapter_up, value_weight, returns, targets)
    return (down.astype(F32)[None], up.astype(F32)[None])


def solution(mesh):
    return jax.shard_map(
        shards,
        mesh=mesh,
        in_specs=(
            P(None, "dp", None),
            P(None, "dp"),
            P("pipe", None, None),
            P("pipe", None, None),
            P(),
            P(),
        ),
        out_specs=(P("pipe", "dp", None), P("pipe", None, "dp")),
        check_vma=False,
    )
```

```python
import functools

import jax
import jax.numpy as jnp
from jax import lax
from jax.experimental import pallas as pl
from jax.experimental.pallas import tpu as pltpu
from jax.sharding import PartitionSpec as P

LAYERS = 8
ZN = 4
TOK = 128
OWN = TOK // ZN
CH = 2048
RANK = 256
FEAT = 8192
TILE = 512
F32 = jnp.float32
BF16 = jnp.bfloat16
MESH = pl.DeviceIdType.MESH


def split3(row):
    hi = row.astype(BF16)
    rest = row - hi.astype(F32)
    mid = rest.astype(BF16)
    lo = (rest - mid.astype(F32)).astype(BF16)
    return [hi.astype(F32), mid.astype(F32), lo.astype(F32)]


def pack_rows(rows):
    parts = []
    for row in rows:
        parts += split3(row)
    at = lax.broadcasted_iota(jnp.int32, (16, 128), 0)
    tile = jnp.zeros((16, 128), F32)
    for i, part in enumerate(parts):
        tile = jnp.where(at == i, jnp.broadcast_to(part, (16, 128)), tile)
    return tile.astype(BF16)


def column(row):
    return jnp.transpose(jnp.broadcast_to(row, (TOK, 128)))


def row_sums(acc):
    return jnp.sum(jnp.transpose(acc), axis=0, keepdims=True)


def fold_lanes(tile):
    total = tile[:, 0:128]
    for i in range(1, tile.shape[1] // 128):
        total = total + tile[:, 128 * i : 128 * (i + 1)]
    return total


def wide(col, width):
    return jnp.concatenate([col] * (width // 128), axis=1)


def dot(a, b):
    return lax.dot_general(a, b, (((1,), (0,)), ((), ())), preferred_element_type=F32)


def dot_nt(a, b):
    return lax.dot_general(a, b, (((1,), (1,)), ((), ())), preferred_element_type=F32)


def dot_tn(a, b):
    return lax.dot_general(a, b, (((0,), (0,)), ((), ())), preferred_element_type=F32)


def kernel(
    x_hbm, wd_hbm, wu_hbm, vw_hbm, ret_hbm, targets_ref, down_ref, up_ref,
    vw_s, ret_s,
    xs, wd, wu, snd, rcv, mine, gx, pre_s, act_s, scale_s,
    gbuf, cbuf, dsum, usum, m1, d1, u1, d2s, u2s, d2, u2, d3s, u3s, res,
    x_ssem, x_rsem, lsem, wsem, ssem, rsem,
    y_ssem, y_rsem, r_ssem, r_rsem, vsem, n_ssem, n_rsem, c_ssem, c_rsem,
    gc_ssem, gc_rsem, gm_ssem, gm_rsem, g1_ssem, g1_rsem, g2_ssem, g2_rsem, g3_ssem, g3_rsem,
):
    dp = lax.axis_index("dp")
    pipe = lax.axis_index("pipe")
    z = dp // 4
    c = lax.rem(dp, 2)
    xh = lax.rem(dp // 2, 2)
    rest = lax.rem(dp, 4)
    xl = pipe // 4
    y = lax.rem(pipe, 4)
    x = xh * 2 + xl
    zs = [lax.rem(z + i, ZN) for i in range(1, ZN)]
    peers = [(zz * 4 + rest, pipe) for zz in zs]
    core_peer = (dp + 1 - 2 * c, pipe)

    def x_dev(xx):
        return (z * 4 + (xx // 2) * 2 + c, lax.rem(xx, 2) * 4 + y)

    def y_dev(yy):
        return (dp, xl * 4 + yy)

    x_at = [lax.rem(x + i, 4) for i in range(1, 4)]
    y_at = [lax.rem(y + i, 4) for i in range(1, 4)]

    def remote(src, dst, send, recv, device):
        return pltpu.make_async_remote_copy(
            src_ref=src, dst_ref=dst, send_sem=send, recv_sem=recv,
            device_id=device, device_id_type=MESH,
        )

    feats = pl.ds(pl.multiple_of(z * CH, CH), CH)
    own_down = pltpu.make_async_copy(wd_hbm.at[0, feats, :], wd.at[pipe], wsem.at[0])
    own_up = pltpu.make_async_copy(wu_hbm.at[0, :, feats], wu.at[pipe], wsem.at[1])
    own_down.start()
    own_up.start()

    def piece(zz):
        return x_hbm.at[y, pl.ds(pl.multiple_of(xl * OWN, OWN), OWN), pl.ds(pl.multiple_of(zz * CH, CH), CH)]

    own_rows = pl.ds(pl.multiple_of(z * OWN, OWN), OWN)
    own = pltpu.make_async_copy(piece(z), xs.at[0, own_rows], lsem)
    own.start()
    small = pltpu.make_async_copy(vw_hbm.at[feats], vw_s.at[0], vsem.at[4])
    small.start()
    ret_copies = [
        pltpu.make_async_copy(ret_hbm.at[pl.ds(128 * i, 128)], ret_s.at[i], vsem.at[i]) for i in range(4)
    ]
    for copy in ret_copies:
        copy.start()

    barrier = pltpu.get_barrier_semaphore()
    greet = peers + [core_peer, x_dev(x_at[0]), x_dev(x_at[1]), x_dev(x_at[2])]
    greet += [(dp, lax.rem(pipe + i, LAYERS)) for i in range(1, LAYERS)]
    for device in greet:
        pl.semaphore_signal(barrier, inc=1, device_id=device, device_id_type=MESH)
    pl.semaphore_wait(barrier, len(greet))

    HALF = CH // 2
    QUART = CH // 4

    def y_copy(which, i, layer):
        at = pl.ds(pl.multiple_of(c * HALF, HALF), HALF)
        far = pl.ds(pl.multiple_of(z * CH + c * HALF, HALF), HALF)
        if which == 0:
            src, dst = wd_hbm.at[0, far, :], wd.at[layer, at, :]
        else:
            src, dst = wu_hbm.at[0, :, far], wu.at[layer, :, at]
        return remote(src, dst, y_ssem.at[which, i], y_rsem.at[which, layer], y_dev(y_at[i]))

    def quarter(which, layer, h):
        at = pl.ds(pl.multiple_of(c * HALF + h * QUART, QUART), QUART)
        return wd.at[layer, at, :] if which == 0 else wu.at[layer, :, at]

    def r_copy(which, layer, h):
        ref = quarter(which, layer, h)
        return remote(ref, ref, r_ssem.at[which, h], r_rsem.at[which, h], y_dev(y_at[2 * h]))

    def n_copy(which, layer, h):
        ref = quarter(which, layer, h)
        return remote(ref, ref, n_ssem.at[which, layer, h], n_rsem.at[which, layer, h], x_dev(x_at[2 * h]))

    def c_copy(which, layer):
        at = pl.ds(pl.multiple_of(c * HALF, HALF), HALF)
        ref = wd.at[layer, at, :] if which == 0 else wu.at[layer, :, at]
        return remote(ref, ref, c_ssem.at[which, layer], c_rsem.at[which, layer], core_peer)

    copies = []
    for i in range(ZN - 1):
        copy = remote(piece(zs[i]), xs.at[0, own_rows], x_ssem.at[i], x_rsem.at[i], peers[i])
        copy.start()
        copies.append(copy)
    def start_own(which):
        for i in (0, 2):
            y_copy(which, i, pipe).start()
        (own_down if which == 0 else own_up).wait()
        if which == 0:
            for h in (0, 1):
                n_copy(which, pipe, h).start()
        else:

            @pl.when(y < 2)
            def _():
                for h in (0, 1):
                    n_copy(1, pipe, h).start()

    start_own(0)

    def column_layer(i):
        return xl * 4 + y_at[i]

    def spread(which):
        for i, h in ((2, 0), (0, 1)):
            layer = column_layer(i)
            y_copy(which, 0, layer).wait_recv()
            r_copy(which, layer, h).start()
            c_copy(which, layer).start()
        for j in range(4):
            layer = xl * 4 + j

            @pl.when(y_at[1] == j)
            def _():
                for h in (0, 1):
                    r_copy(which, layer, h).wait_recv()
                    n_copy(which, layer, h).start()
                c_copy(which, layer).start()

            later = (y == j) & (j >= 2) if which == 1 else False
            @pl.when((y != j) & (y_at[1] != j) | later)
            def _():
                for h in (0, 1):
                    n_copy(which, layer, h).start()

    def pass_on(which, layer):
        @pl.when(layer // 4 != xl)
        def _():
            n_copy(which, layer, 0).wait_recv()
            n_copy(which, layer, 1).wait_recv()
            c_copy(which, layer).start()

    def wait_weights(which, layer):
        @pl.when(layer != pipe)
        def _():
            c_copy(which, layer).wait_recv()

    def sent_weights(which, layer):
        @pl.when(layer // 4 == xl)
        def _():
            n_copy(which, layer, 0).wait_send()
            n_copy(which, layer, 1).wait_send()

        @pl.when(layer != pipe)
        def _():
            c_copy(which, layer).wait_send()

    def exchange(slot, rows):
        return [
            remote(
                snd.at[slot, pl.ds(0, rows)], rcv.at[slot, i, pl.ds(0, rows)],
                ssem.at[slot, i], rsem.at[slot, i], peers[i],
            )
            for i in range(ZN - 1)
        ]

    def begin(copies):
        for copy in copies:
            copy.start()

    def begin_exchange(slot, rows):
        first, far, last = exchange(slot, rows)
        begin([far, first, last])

    def finish(copies):
        for copy in copies:
            copy.wait()

    def cols(t):
        return slice(t * TILE, (t + 1) * TILE)

    def send_product(slot, product, square):
        mine[...] = product
        snd[slot, 16 : 16 + TOK] = product.astype(BF16)
        row = row_sums(square)
        snd[slot, 0:16, 0:128] = pack_rows([row])
        return row

    def row_total(slot, first, own_row):
        total = own_row
        for i in range(ZN - 1):
            part = rcv[slot, i, 0:16, 0:128].astype(F32)[first : first + 3]
            total = total + jnp.sum(part, axis=0, keepdims=True)
        return total

    snd[...] = jnp.zeros_like(snd)
    wanted = targets_ref[pl.ds(y, 1), :].astype(F32)
    wanted = column(jnp.concatenate([wanted, jnp.zeros_like(wanted)], axis=1))
    lane = lax.broadcasted_iota(jnp.int32, (TOK, 128), 1)
    small.wait()
    for copy in ret_copies:
        copy.wait()
    found = jnp.zeros((TOK, 128), F32)
    for i in range(4):
        agent = (lane + 128 * i).astype(F32)
        found += jnp.where(wanted == agent, jnp.broadcast_to(ret_s[i : i + 1, :], (TOK, 128)), 0.0)
    target_tile = pltpu.roll(
        jnp.broadcast_to(row_sums(found), (8, 128)), lax.rem(z * OWN + 128 - xl * OWN, 128), axis=1
    )
    target_tile = jnp.where((lane[:8] >= z * OWN) & (lane[:8] < z * OWN + OWN), target_tile, 0.0)
    target_row = target_tile[0:1]
    spread(0)
    own.wait()
    finish(copies)
    start_own(1)
    pass_on(0, 0)
    wait_weights(0, 0)
    product = jnp.zeros((TOK, RANK), F32)
    square = jnp.zeros((TOK, 128), F32)
    for t in range(CH // TILE):
        tile = xs[0, :, cols(t)]
        wide_tile = tile.astype(F32)
        square += fold_lanes(wide_tile * wide_tile)
        product += dot(tile, wd[0, cols(t), :])
    own_row = send_product(0, product, square)

    def forward(layer, own_row):
        slot = lax.rem(layer, 2)
        begin_exchange(slot, 16 + TOK)

        @pl.when(layer == 0)
        def _():
            pass_on(0, 1)
            spread(1)
            pass_on(1, 0)

        @pl.when(layer < LAYERS - 1)
        def _():
            pass_on(1, layer + 1)

        @pl.when(layer < LAYERS - 2)
        def _():
            pass_on(0, layer + 2)

        finish(exchange(slot, 16 + TOK))
        total = mine[...]
        for i in range(ZN - 1):
            total = total + rcv[slot, i, 16 : 16 + TOK].astype(F32)
        ssq = row_total(slot, 0, own_row)
        scale = column(lax.rsqrt(ssq * (1.0 / FEAT) + 1e-05))
        pre = total * wide(scale, RANK)
        act = (pre / (1.0 + jnp.exp(-pre))).astype(BF16)
        scale_s[layer] = scale
        pre_s[layer] = pre
        act_s[layer] = act
        after = jnp.minimum(layer + 1, LAYERS - 1)
        wait_weights(1, layer)

        @pl.when(layer < LAYERS - 1)
        def _():
            wait_weights(0, layer + 1)

        product = jnp.zeros((TOK, RANK), F32)
        square = jnp.zeros((TOK, 128), F32)
        for t in range(CH // TILE):
            tile = (xs[layer, :, cols(t)].astype(F32) + dot(act, wu[layer, :, cols(t)])).astype(BF16)
            xs[layer + 1, :, cols(t)] = tile
            wide_tile = tile.astype(F32)
            square += fold_lanes(wide_tile * wide_tile)
            product += dot(tile, wd[after, cols(t), :])
        return send_product(1 - slot, product, square)

    own_row = lax.fori_loop(0, LAYERS, forward, own_row)

    value_acc = jnp.zeros((TOK, 128), F32)
    for t in range(CH // TILE):
        weight = vw_s[0:1, cols(t)]
        value_acc += fold_lanes(xs[LAYERS, :, cols(t)].astype(F32) * weight)
    value_row = row_sums(value_acc)
    snd[0, 0:16, 0:128] = pack_rows([own_row, value_row, target_row])
    begin_exchange(0, 16)
    for which in (0, 1):
        for i in (0, 2):
            y_copy(which, i, pipe).wait_send()
        for h in (0, 1):
            r_copy(which, pipe, h).wait_send()
        for layer in range(LAYERS):
            sent_weights(which, layer)
    finish(exchange(0, 16))
    ssq = row_total(0, 0, own_row)
    raw = row_total(0, 3, value_row)
    target = row_total(0, 6, target_row)
    scale = lax.rsqrt(ssq * (1.0 / FEAT) + 1e-05)
    value = scale * raw
    resid = value - target
    on_weight = column(scale * resid)
    on_x = column(-scale * scale * resid * value * (1.0 / FEAT))
    product = jnp.zeros((TOK, RANK), F32)
    for t in range(CH // TILE):
        weight = vw_s[0:1, cols(t)]
        tile = (
            wide(on_weight, TILE) * weight + wide(on_x, TILE) * xs[LAYERS, :, cols(t)].astype(F32)
        ).astype(BF16)
        gx[0, :, cols(t)] = tile
        product += dot_nt(tile, wu[LAYERS - 1, :, cols(t)])
    mine[...] = product
    snd[1, 16 : 16 + TOK] = product.astype(BF16)
    begin_exchange(1, 16 + TOK)

    def core_copy(layer, half):
        slot = lax.rem(layer, 2)
        return remote(
            gbuf.at[slot, 2 * half + 1 - c], cbuf.at[layer, half],
            gc_ssem.at[slot, half], gc_rsem.at[layer, half], core_peer,
        )

    def middle_copies(layer):
        deep = lax.rem(layer, 4)
        found = []
        for k, i in ((0, 0), (1, 2)):
            found.append(remote(
                dsum.at[deep, x_at[1], pl.ds(2 * k, 2)], m1.at[0, layer, k],
                gm_ssem.at[deep, 0, k], gm_rsem.at[layer, 0, k], x_dev(x_at[i]),
            ))
            found.append(remote(
                usum.at[deep, y_at[1], pl.ds(2 * k, 2)], m1.at[1, layer, k],
                gm_ssem.at[deep, 1, k], gm_rsem.at[layer, 1, k], y_dev(y_at[i]),
            ))
        return found

    def first_copies(layer):
        deep = lax.rem(layer, 4)
        found = []
        for k, i in ((0, 0), (1, 2)):
            found.append(remote(
                dsum.at[deep, x_at[i]], d1.at[layer, k],
                g1_ssem.at[deep, 0, k], g1_rsem.at[layer, 0, k], x_dev(x_at[i]),
            ))
            found.append(remote(
                usum.at[deep, y_at[i]], u1.at[layer, k],
                g1_ssem.at[deep, 1, k], g1_rsem.at[layer, 1, k], y_dev(y_at[i]),
            ))
        return found

    def second_copies(layer):
        slot = lax.rem(layer, 2)
        found = []
        for i in range(3):
            found.append(remote(
                d2s.at[slot, y_at[i]], d2.at[layer, i],
                g2_ssem.at[slot, 0, i], g2_rsem.at[layer, 0, i], y_dev(y_at[i]),
            ))
            found.append(remote(
                u2s.at[slot, x_at[i]], u2.at[layer, i],
                g2_ssem.at[slot, 1, i], g2_rsem.at[layer, 1, i], x_dev(x_at[i]),
            ))
        return found

    def last_copies(layer):
        return [
            remote(src.at[layer], res.at[which, pipe], g3_ssem.at[layer, which], g3_rsem.at[which, pipe], (dp, layer))
            for which, src in ((0, d3s), (1, u3s))
        ]

    def add_cores(layer):
        slot = lax.rem(layer, 2)
        for half in (0, 1):
            core_copy(layer, half).wait()
        deep = lax.rem(layer, 4)
        for half in (0, 1):
            for block in range(2):
                for part in range(4):
                    at = slice(block * 128 + part * 32, block * 128 + part * 32 + 32)
                    dsum[deep, 2 * half + block, part] = (
                        gbuf[slot, 2 * half + c, at].astype(F32) + cbuf[layer, half, at].astype(F32)
                    ).astype(BF16)
                    at = slice(RANK + at.start, RANK + at.stop)
                    usum[deep, part, 2 * half + block] = (
                        gbuf[slot, 2 * half + c, at].astype(F32) + cbuf[layer, half, at].astype(F32)
                    ).astype(BF16)
        begin(middle_copies(layer))

    def add_middle(layer):
        deep = lax.rem(layer, 4)
        finish(middle_copies(layer))
        for k, i in ((0, 0), (1, 2)):
            for part in range(2):
                for which, total, at in ((0, dsum, x_at[i]), (1, usum, y_at[i])):
                    total[deep, at, 2 * k + part] = (
                        total[deep, at, 2 * k + part].astype(F32) + m1[which, layer, k, part].astype(F32)
                    ).astype(BF16)
        begin(first_copies(layer))

    def add_first(layer):
        slot = lax.rem(layer, 2)
        finish(first_copies(layer))
        for part in range(4):
            for total, at, got, to in ((dsum, x, d1, d2s), (usum, y, u1, u2s)):
                value = total[lax.rem(layer, 4), at, part].astype(F32)
                for i in range(2):
                    value = value + got[layer, i, part].astype(F32)
                to[slot, part] = value.astype(BF16)
        begin(second_copies(layer))

    def add_second(layer):
        slot = lax.rem(layer, 2)
        finish(second_copies(layer))
        done = []
        for total, at, got in ((d2s, y, d2), (u2s, x, u2)):
            value = total[slot, at].astype(F32)
            for i in range(3):
                value = value + got[layer, i].astype(F32)
            done.append(value.astype(BF16))

        @pl.when(layer == pipe)
        def _():
            res[0, pipe] = done[0]
            res[1, pipe] = done[1]

        @pl.when(layer != pipe)
        def _():
            d3s[layer] = done[0]
            u3s[layer] = done[1]
            begin(last_copies(layer))

    def sums(step):
        @pl.when((step >= 1) & (step < LAYERS + 1))
        def _():
            add_cores(LAYERS - step)

        @pl.when((step >= 2) & (step < LAYERS + 2))
        def _():
            add_middle(LAYERS + 1 - step)

        @pl.when((step >= 3) & (step < LAYERS + 3))
        def _():
            add_first(LAYERS + 2 - step)

        @pl.when(step >= 4)
        def _():
            add_second(LAYERS + 3 - step)

    def backward(step, carry):
        layer = LAYERS - 1 - step
        slot = lax.rem(step + 1, 2)
        now = lax.rem(step, 2)
        finish(exchange(slot, 16 + TOK))
        total = mine[...]
        for i in range(ZN - 1):
            total = total + rcv[slot, i, 16 : 16 + TOK].astype(F32)
        pre = pre_s[layer]
        scale = scale_s[layer]
        sigma = 1.0 / (1.0 + jnp.exp(-pre))
        grad_pre = (total * sigma * (1.0 + pre * (1.0 - sigma))).astype(BF16)
        grad_f = grad_pre.astype(F32)
        inner = jnp.sum(grad_f * pre, axis=1, keepdims=True) * (1.0 / FEAT)
        scaled = (grad_f * wide(scale, RANK)).astype(BF16)

        @pl.when(layer > 0)
        def _():
            on_x = wide(scale * scale * inner, TILE)
            on_q = wide(scale, TILE)
            product = jnp.zeros((TOK, RANK), F32)
            for t in range(CH // TILE):
                q = dot_nt(grad_pre, wd[layer, cols(t), :])
                tile = (
                    gx[now, :, cols(t)].astype(F32) + on_q * q - on_x * xs[layer, :, cols(t)].astype(F32)
                ).astype(BF16)
                gx[1 - now, :, cols(t)] = tile
                product += dot_nt(tile, wu[layer - 1, :, cols(t)])
            mine[...] = product
            snd[1 - slot, 16 : 16 + TOK] = product.astype(BF16)
            begin_exchange(1 - slot, 16 + TOK)

        act = act_s[layer]
        turn = lax.rem(layer, 2)
        for t in range(CH // TILE):
            gbuf[turn, t, 0:RANK] = dot_tn(scaled, xs[layer, :, cols(t)]).astype(BF16)
            gbuf[turn, t, RANK : 2 * RANK] = dot_tn(act, gx[now, :, cols(t)]).astype(BF16)
        for half in (0, 1):
            core_copy(layer, half).start()
        sums(step)
        return carry

    lax.fori_loop(0, LAYERS, backward, 0)

    def rest_of_sums(step, carry):
        sums(step)
        return carry

    lax.fori_loop(LAYERS, LAYERS + 4, rest_of_sums, 0)

    def finish_last(layer, carry):
        @pl.when(layer != pipe)
        def _():
            for copy in last_copies(layer):
                copy.wait_send()
            for which in (0, 1):
                remote(
                    d3s.at[layer], res.at[which, layer],
                    g3_ssem.at[layer, which], g3_rsem.at[which, layer], (dp, layer),
                ).wait_recv()
        return carry

    lax.fori_loop(0, LAYERS, finish_last, 0)
    down = jnp.concatenate([res[0, part].astype(F32) for part in range(LAYERS)], axis=0)
    down_ref[...] = jnp.transpose(down).astype(BF16)
    for part in range(LAYERS):
        up_ref[part * 32 : part * 32 + 32] = res[1, part]


def shards(inputs, targets, adapter_down, adapter_up, value_weight, returns):
    any_spec = pl.BlockSpec(memory_space=pl.ANY)
    vmem = pl.BlockSpec(memory_space=pltpu.VMEM)
    dma = pltpu.SemaphoreType.DMA
    down, up = pl.pallas_call(
        kernel,
        out_shape=(
            jax.ShapeDtypeStruct((TILE, RANK), BF16),
            jax.ShapeDtypeStruct((RANK, TILE), BF16),
        ),
        in_specs=[any_spec, any_spec, any_spec, any_spec, any_spec, vmem],
        out_specs=(vmem, vmem),
        scratch_shapes=[
            pltpu.VMEM((8, CH), F32),
            pltpu.VMEM((8, 128), F32),
            pltpu.VMEM((LAYERS + 1, TOK, CH), BF16),
            pltpu.VMEM((LAYERS, CH, RANK), BF16),
            pltpu.VMEM((LAYERS, RANK, CH), BF16),
            pltpu.VMEM((2, 16 + TOK, RANK), BF16),
            pltpu.VMEM((2, ZN - 1, 16 + TOK, RANK), BF16),
            pltpu.VMEM((TOK, RANK), F32),
            pltpu.VMEM((2, TOK, CH), BF16),
            pltpu.VMEM((LAYERS, TOK, RANK), F32),
            pltpu.VMEM((LAYERS, TOK, RANK), BF16),
            pltpu.VMEM((LAYERS, TOK, 128), F32),
            pltpu.VMEM((2, 4, 2 * RANK, TILE), BF16),
            pltpu.VMEM((LAYERS, 2, 2 * RANK, TILE), BF16),
            pltpu.VMEM((4, 4, 4, 32, TILE), BF16),
            pltpu.VMEM((4, 4, 4, 32, TILE), BF16),
            pltpu.VMEM((2, LAYERS, 2, 2, 32, TILE), BF16),
            pltpu.VMEM((LAYERS, 2, 4, 32, TILE), BF16),
            pltpu.VMEM((LAYERS, 2, 4, 32, TILE), BF16),
            pltpu.VMEM((2, 4, 32, TILE), BF16),
            pltpu.VMEM((2, 4, 32, TILE), BF16),
            pltpu.VMEM((LAYERS, 3, 32, TILE), BF16),
            pltpu.VMEM((LAYERS, 3, 32, TILE), BF16),
            pltpu.VMEM((LAYERS, 32, TILE), BF16),
            pltpu.VMEM((LAYERS, 32, TILE), BF16),
            pltpu.VMEM((2, LAYERS, 32, TILE), BF16),
            dma((ZN - 1,)),
            dma((ZN - 1,)),
            dma,
            dma((2,)),
            dma((2, ZN - 1)),
            dma((2, ZN - 1)),
            dma((2, 3)),
            dma((2, LAYERS)),
            dma((2, 2)),
            dma((2, 2)),
            dma((5,)),
            dma((2, LAYERS, 2)),
            dma((2, LAYERS, 2)),
            dma((2, LAYERS)),
            dma((2, LAYERS)),
            dma((2, 2)),
            dma((LAYERS, 2)),
            dma((4, 2, 2)),
            dma((LAYERS, 2, 2)),
            dma((4, 2, 2)),
            dma((LAYERS, 2, 2)),
            dma((2, 2, 3)),
            dma((LAYERS, 2, 3)),
            dma((LAYERS, 2)),
            dma((2, LAYERS)),
        ],
        compiler_params=pltpu.CompilerParams(
            collective_id=0, has_side_effects=True, vmem_limit_bytes=60 * 1024 * 1024
        ),
        name="relay",
    )(inputs, adapter_down, adapter_up, value_weight, returns, targets)
    return (down.astype(F32)[None], up.astype(F32)[None])


def solution(mesh):
    return jax.shard_map(
        shards,
        mesh=mesh,
        in_specs=(
            P(None, "dp", None),
            P(None, "dp"),
            P("pipe", None, None),
            P("pipe", None, None),
            P(),
            P(),
        ),
        out_specs=(P("pipe", "dp", None), P("pipe", None, "dp")),
        check_vma=False,
    )
```

```python
import functools

import jax
import jax.numpy as jnp
from jax import lax
from jax.experimental import pallas as pl
from jax.experimental.pallas import tpu as pltpu
from jax.sharding import PartitionSpec as P

LAYERS = 8
ZN = 4
TOK = 128
OWN = TOK // ZN
CH = 2048
RANK = 256
FEAT = 8192
TILE = 512
F32 = jnp.float32
BF16 = jnp.bfloat16
MESH = pl.DeviceIdType.MESH


def split3(row):
    hi = row.astype(BF16)
    rest = row - hi.astype(F32)
    mid = rest.astype(BF16)
    lo = (rest - mid.astype(F32)).astype(BF16)
    return [hi.astype(F32), mid.astype(F32), lo.astype(F32)]


def pack_rows(rows):
    parts = []
    for row in rows:
        parts += split3(row)
    at = lax.broadcasted_iota(jnp.int32, (16, 128), 0)
    tile = jnp.zeros((16, 128), F32)
    for i, part in enumerate(parts):
        tile = jnp.where(at == i, jnp.broadcast_to(part, (16, 128)), tile)
    return tile.astype(BF16)


def column(row):
    return jnp.transpose(jnp.broadcast_to(row, (TOK, 128)))


def row_sums(acc):
    return jnp.sum(jnp.transpose(acc), axis=0, keepdims=True)


def fold_lanes(tile):
    total = tile[:, 0:128]
    for i in range(1, tile.shape[1] // 128):
        total = total + tile[:, 128 * i : 128 * (i + 1)]
    return total


def wide(col, width):
    return jnp.concatenate([col] * (width // 128), axis=1)


def dot(a, b):
    return lax.dot_general(a, b, (((1,), (0,)), ((), ())), preferred_element_type=F32)


def dot_nt(a, b):
    return lax.dot_general(a, b, (((1,), (1,)), ((), ())), preferred_element_type=F32)


def dot_tn(a, b):
    return lax.dot_general(a, b, (((0,), (0,)), ((), ())), preferred_element_type=F32)


def kernel(
    x_hbm, wd_hbm, wu_hbm, vw_hbm, ret_hbm, targets_ref, down_ref, up_ref,
    vw_s, ret_s,
    xs, wd, wu, snd, rcv, mine, gx, pre_s, act_s, scale_s,
    gbuf, cbuf, dsum, usum, m1, d1, u1, d2s, u2s, d2, u2, d3s, u3s, res,
    x_ssem, x_rsem, lsem, wsem, ssem, rsem,
    y_ssem, y_rsem, r_ssem, r_rsem, vsem, n_ssem, n_rsem, c_ssem, c_rsem,
    gc_ssem, gc_rsem, gm_ssem, gm_rsem, g1_ssem, g1_rsem, g2_ssem, g2_rsem, g3_ssem, g3_rsem,
):
    dp = lax.axis_index("dp")
    pipe = lax.axis_index("pipe")
    z = dp // 4
    c = lax.rem(dp, 2)
    xh = lax.rem(dp // 2, 2)
    rest = lax.rem(dp, 4)
    xl = pipe // 4
    y = lax.rem(pipe, 4)
    x = xh * 2 + xl
    zs = [lax.rem(z + i, ZN) for i in range(1, ZN)]
    peers = [(zz * 4 + rest, pipe) for zz in zs]
    core_peer = (dp + 1 - 2 * c, pipe)

    def x_dev(xx):
        return (z * 4 + (xx // 2) * 2 + c, lax.rem(xx, 2) * 4 + y)

    def y_dev(yy):
        return (dp, xl * 4 + yy)

    x_at = [lax.rem(x + i, 4) for i in range(1, 4)]
    y_at = [lax.rem(y + i, 4) for i in range(1, 4)]

    def remote(src, dst, send, recv, device):
        return pltpu.make_async_remote_copy(
            src_ref=src, dst_ref=dst, send_sem=send, recv_sem=recv,
            device_id=device, device_id_type=MESH,
        )

    feats = pl.ds(pl.multiple_of(z * CH, CH), CH)
    own_down = pltpu.make_async_copy(wd_hbm.at[0, feats, :], wd.at[pipe], wsem.at[0])
    own_up = pltpu.make_async_copy(wu_hbm.at[0, :, feats], wu.at[pipe], wsem.at[1])
    own_down.start()
    own_up.start()

    def piece(zz):
        return x_hbm.at[y, pl.ds(pl.multiple_of(xl * OWN, OWN), OWN), pl.ds(pl.multiple_of(zz * CH, CH), CH)]

    own_rows = pl.ds(pl.multiple_of(z * OWN, OWN), OWN)
    own = pltpu.make_async_copy(piece(z), xs.at[0, own_rows], lsem)
    own.start()
    small = pltpu.make_async_copy(vw_hbm.at[feats], vw_s.at[0], vsem.at[4])
    small.start()
    ret_copies = [
        pltpu.make_async_copy(ret_hbm.at[pl.ds(128 * i, 128)], ret_s.at[i], vsem.at[i]) for i in range(4)
    ]
    for copy in ret_copies:
        copy.start()

    barrier = pltpu.get_barrier_semaphore()
    greet = peers + [core_peer, x_dev(x_at[0]), x_dev(x_at[1]), x_dev(x_at[2])]
    greet += [(dp, lax.rem(pipe + i, LAYERS)) for i in range(1, LAYERS)]
    for device in greet:
        pl.semaphore_signal(barrier, inc=1, device_id=device, device_id_type=MESH)
    pl.semaphore_wait(barrier, len(greet))

    HALF = CH // 2
    QUART = CH // 4

    def y_copy(which, i, layer):
        at = pl.ds(pl.multiple_of(c * HALF, HALF), HALF)
        far = pl.ds(pl.multiple_of(z * CH + c * HALF, HALF), HALF)
        if which == 0:
            src, dst = wd_hbm.at[0, far, :], wd.at[layer, at, :]
        else:
            src, dst = wu_hbm.at[0, :, far], wu.at[layer, :, at]
        return remote(src, dst, y_ssem.at[which, i], y_rsem.at[which, layer], y_dev(y_at[i]))

    def quarter(which, layer, h):
        at = pl.ds(pl.multiple_of(c * HALF + h * QUART, QUART), QUART)
        return wd.at[layer, at, :] if which == 0 else wu.at[layer, :, at]

    def r_copy(which, layer, h):
        ref = quarter(which, layer, h)
        return remote(ref, ref, r_ssem.at[which, h], r_rsem.at[which, h], y_dev(y_at[2 * h]))

    def n_copy(which, layer, h):
        ref = quarter(which, layer, h)
        return remote(ref, ref, n_ssem.at[which, layer, h], n_rsem.at[which, layer, h], x_dev(x_at[2 * h]))

    def c_copy(which, layer):
        at = pl.ds(pl.multiple_of(c * HALF, HALF), HALF)
        ref = wd.at[layer, at, :] if which == 0 else wu.at[layer, :, at]
        return remote(ref, ref, c_ssem.at[which, layer], c_rsem.at[which, layer], core_peer)

    copies = []
    for i in range(ZN - 1):
        copy = remote(piece(zs[i]), xs.at[0, own_rows], x_ssem.at[i], x_rsem.at[i], peers[i])
        copy.start()
        copies.append(copy)
    def start_own(which):
        for i in (0, 2):
            y_copy(which, i, pipe).start()
        (own_down if which == 0 else own_up).wait()
        if which == 0:
            for h in (0, 1):
                n_copy(which, pipe, h).start()
        else:

            @pl.when(y < 2)
            def _():
                for h in (0, 1):
                    n_copy(1, pipe, h).start()

    start_own(0)

    def column_layer(i):
        return xl * 4 + y_at[i]

    def spread(which):
        for i, h in ((2, 0), (0, 1)):
            layer = column_layer(i)
            y_copy(which, 0, layer).wait_recv()
            r_copy(which, layer, h).start()
            c_copy(which, layer).start()
        for j in range(4):
            layer = xl * 4 + j

            @pl.when(y_at[1] == j)
            def _():
                for h in (0, 1):
                    r_copy(which, layer, h).wait_recv()
                    n_copy(which, layer, h).start()
                c_copy(which, layer).start()

            later = (y == j) & (j >= 2) if which == 1 else False
            @pl.when((y != j) & (y_at[1] != j) | later)
            def _():
                for h in (0, 1):
                    n_copy(which, layer, h).start()

    def pass_on(which, layer):
        @pl.when(layer // 4 != xl)
        def _():
            n_copy(which, layer, 0).wait_recv()
            n_copy(which, layer, 1).wait_recv()
            c_copy(which, layer).start()

    def wait_weights(which, layer):
        @pl.when(layer != pipe)
        def _():
            c_copy(which, layer).wait_recv()

    def sent_weights(which, layer):
        @pl.when(layer // 4 == xl)
        def _():
            n_copy(which, layer, 0).wait_send()
            n_copy(which, layer, 1).wait_send()

        @pl.when(layer != pipe)
        def _():
            c_copy(which, layer).wait_send()

    def exchange(slot, rows):
        return [
            remote(
                snd.at[slot, pl.ds(0, rows)], rcv.at[slot, i, pl.ds(0, rows)],
                ssem.at[slot, i], rsem.at[slot, i], peers[i],
            )
            for i in range(ZN - 1)
        ]

    def begin(copies):
        for copy in copies:
            copy.start()

    def begin_exchange(slot, rows):
        first, far, last = exchange(slot, rows)
        begin([far, first, last])

    def finish(copies):
        for copy in copies:
            copy.wait()

    def cols(t):
        return slice(t * TILE, (t + 1) * TILE)

    def send_product(slot, product, square):
        mine[...] = product
        snd[slot, 16 : 16 + TOK] = product.astype(BF16)
        row = row_sums(square)
        snd[slot, 0:16, 0:128] = pack_rows([row])
        return row

    def row_total(slot, first, own_row):
        total = own_row
        for i in range(ZN - 1):
            part = rcv[slot, i, 0:16, 0:128].astype(F32)[first : first + 3]
            total = total + jnp.sum(part, axis=0, keepdims=True)
        return total

    snd[...] = jnp.zeros_like(snd)
    own.wait()
    finish(copies)
    wanted = targets_ref[pl.ds(y, 1), :].astype(F32)
    wanted = column(jnp.concatenate([wanted, jnp.zeros_like(wanted)], axis=1))
    lane = lax.broadcasted_iota(jnp.int32, (TOK, 128), 1)
    small.wait()
    for copy in ret_copies:
        copy.wait()
    found = jnp.zeros((TOK, 128), F32)
    for i in range(4):
        agent = (lane + 128 * i).astype(F32)
        found += jnp.where(wanted == agent, jnp.broadcast_to(ret_s[i : i + 1, :], (TOK, 128)), 0.0)
    target_tile = pltpu.roll(
        jnp.broadcast_to(row_sums(found), (8, 128)), lax.rem(z * OWN + 128 - xl * OWN, 128), axis=1
    )
    target_tile = jnp.where((lane[:8] >= z * OWN) & (lane[:8] < z * OWN + OWN), target_tile, 0.0)
    target_row = target_tile[0:1]
    spread(0)
    start_own(1)
    pass_on(0, 0)
    wait_weights(0, 0)
    product = jnp.zeros((TOK, RANK), F32)
    square = jnp.zeros((TOK, 128), F32)
    for t in range(CH // TILE):
        tile = xs[0, :, cols(t)]
        wide_tile = tile.astype(F32)
        square += fold_lanes(wide_tile * wide_tile)
        product += dot(tile, wd[0, cols(t), :])
    own_row = send_product(0, product, square)

    def forward(layer, own_row):
        slot = lax.rem(layer, 2)
        begin_exchange(slot, 16 + TOK)

        @pl.when(layer == 0)
        def _():
            spread(1)

        pass_on(1, layer)

        @pl.when(layer < LAYERS - 1)
        def _():
            pass_on(0, layer + 1)

        finish(exchange(slot, 16 + TOK))
        total = mine[...]
        for i in range(ZN - 1):
            total = total + rcv[slot, i, 16 : 16 + TOK].astype(F32)
        ssq = row_total(slot, 0, own_row)
        scale = column(lax.rsqrt(ssq * (1.0 / FEAT) + 1e-05))
        pre = total * wide(scale, RANK)
        act = (pre / (1.0 + jnp.exp(-pre))).astype(BF16)
        scale_s[layer] = scale
        pre_s[layer] = pre
        act_s[layer] = act
        after = jnp.minimum(layer + 1, LAYERS - 1)
        wait_weights(1, layer)

        @pl.when(layer < LAYERS - 1)
        def _():
            wait_weights(0, layer + 1)

        product = jnp.zeros((TOK, RANK), F32)
        square = jnp.zeros((TOK, 128), F32)
        for t in range(CH // TILE):
            tile = (xs[layer, :, cols(t)].astype(F32) + dot(act, wu[layer, :, cols(t)])).astype(BF16)
            xs[layer + 1, :, cols(t)] = tile
            wide_tile = tile.astype(F32)
            square += fold_lanes(wide_tile * wide_tile)
            product += dot(tile, wd[after, cols(t), :])
        return send_product(1 - slot, product, square)

    own_row = lax.fori_loop(0, LAYERS, forward, own_row)

    value_acc = jnp.zeros((TOK, 128), F32)
    for t in range(CH // TILE):
        weight = vw_s[0:1, cols(t)]
        value_acc += fold_lanes(xs[LAYERS, :, cols(t)].astype(F32) * weight)
    value_row = row_sums(value_acc)
    snd[0, 0:16, 0:128] = pack_rows([own_row, value_row, target_row])
    begin_exchange(0, 16)
    for which in (0, 1):
        for i in (0, 2):
            y_copy(which, i, pipe).wait_send()
        for h in (0, 1):
            r_copy(which, pipe, h).wait_send()
        for layer in range(LAYERS):
            sent_weights(which, layer)
    finish(exchange(0, 16))
    ssq = row_total(0, 0, own_row)
    raw = row_total(0, 3, value_row)
    target = row_total(0, 6, target_row)
    scale = lax.rsqrt(ssq * (1.0 / FEAT) + 1e-05)
    value = scale * raw
    resid = value - target
    on_weight = column(scale * resid)
    on_x = column(-scale * scale * resid * value * (1.0 / FEAT))
    product = jnp.zeros((TOK, RANK), F32)
    for t in range(CH // TILE):
        weight = vw_s[0:1, cols(t)]
        tile = (
            wide(on_weight, TILE) * weight + wide(on_x, TILE) * xs[LAYERS, :, cols(t)].astype(F32)
        ).astype(BF16)
        gx[0, :, cols(t)] = tile
        product += dot_nt(tile, wu[LAYERS - 1, :, cols(t)])
    mine[...] = product
    snd[1, 16 : 16 + TOK] = product.astype(BF16)
    begin_exchange(1, 16 + TOK)

    def core_copy(layer, half):
        slot = lax.rem(layer, 2)
        return remote(
            gbuf.at[slot, 2 * half + 1 - c], cbuf.at[layer, half],
            gc_ssem.at[slot, half], gc_rsem.at[layer, half], core_peer,
        )

    def middle_copies(layer):
        deep = lax.rem(layer, 4)
        found = []
        for k, i in ((0, 0), (1, 2)):
            found.append(remote(
                dsum.at[deep, x_at[1], pl.ds(2 * k, 2)], m1.at[0, layer, k],
                gm_ssem.at[deep, 0, k], gm_rsem.at[layer, 0, k], x_dev(x_at[i]),
            ))
            found.append(remote(
                usum.at[deep, y_at[1], pl.ds(2 * k, 2)], m1.at[1, layer, k],
                gm_ssem.at[deep, 1, k], gm_rsem.at[layer, 1, k], y_dev(y_at[i]),
            ))
        return found

    def first_copies(layer):
        deep = lax.rem(layer, 4)
        found = []
        for k, i in ((0, 0), (1, 2)):
            found.append(remote(
                dsum.at[deep, x_at[i]], d1.at[layer, k],
                g1_ssem.at[deep, 0, k], g1_rsem.at[layer, 0, k], x_dev(x_at[i]),
            ))
            found.append(remote(
                usum.at[deep, y_at[i]], u1.at[layer, k],
                g1_ssem.at[deep, 1, k], g1_rsem.at[layer, 1, k], y_dev(y_at[i]),
            ))
        return found

    def second_copies(layer):
        slot = lax.rem(layer, 2)
        found = []
        for i in range(3):
            found.append(remote(
                d2s.at[slot, y_at[i]], d2.at[layer, i],
                g2_ssem.at[slot, 0, i], g2_rsem.at[layer, 0, i], y_dev(y_at[i]),
            ))
            found.append(remote(
                u2s.at[slot, x_at[i]], u2.at[layer, i],
                g2_ssem.at[slot, 1, i], g2_rsem.at[layer, 1, i], x_dev(x_at[i]),
            ))
        return found

    def last_copies(layer):
        return [
            remote(src.at[layer], res.at[which, pipe], g3_ssem.at[layer, which], g3_rsem.at[which, pipe], (dp, layer))
            for which, src in ((0, d3s), (1, u3s))
        ]

    def add_cores(layer):
        slot = lax.rem(layer, 2)
        for half in (0, 1):
            core_copy(layer, half).wait()
        deep = lax.rem(layer, 4)
        for half in (0, 1):
            for block in range(2):
                for part in range(4):
                    at = slice(block * 128 + part * 32, block * 128 + part * 32 + 32)
                    dsum[deep, 2 * half + block, part] = (
                        gbuf[slot, 2 * half + c, at].astype(F32) + cbuf[layer, half, at].astype(F32)
                    ).astype(BF16)
                    at = slice(RANK + at.start, RANK + at.stop)
                    usum[deep, part, 2 * half + block] = (
                        gbuf[slot, 2 * half + c, at].astype(F32) + cbuf[layer, half, at].astype(F32)
                    ).astype(BF16)
        begin(middle_copies(layer))

    def add_middle(layer):
        deep = lax.rem(layer, 4)
        finish(middle_copies(layer))
        for k, i in ((0, 0), (1, 2)):
            for part in range(2):
                for which, total, at in ((0, dsum, x_at[i]), (1, usum, y_at[i])):
                    total[deep, at, 2 * k + part] = (
                        total[deep, at, 2 * k + part].astype(F32) + m1[which, layer, k, part].astype(F32)
                    ).astype(BF16)
        begin(first_copies(layer))

    def add_first(layer):
        slot = lax.rem(layer, 2)
        finish(first_copies(layer))
        for part in range(4):
            for total, at, got, to in ((dsum, x, d1, d2s), (usum, y, u1, u2s)):
                value = total[lax.rem(layer, 4), at, part].astype(F32)
                for i in range(2):
                    value = value + got[layer, i, part].astype(F32)
                to[slot, part] = value.astype(BF16)
        begin(second_copies(layer))

    def add_second(layer):
        slot = lax.rem(layer, 2)
        finish(second_copies(layer))
        done = []
        for total, at, got in ((d2s, y, d2), (u2s, x, u2)):
            value = total[slot, at].astype(F32)
            for i in range(3):
                value = value + got[layer, i].astype(F32)
            done.append(value.astype(BF16))

        @pl.when(layer == pipe)
        def _():
            res[0, pipe] = done[0]
            res[1, pipe] = done[1]

        @pl.when(layer != pipe)
        def _():
            d3s[layer] = done[0]
            u3s[layer] = done[1]
            begin(last_copies(layer))

    def sums(step):
        @pl.when((step >= 1) & (step < LAYERS + 1))
        def _():
            add_cores(LAYERS - step)

        @pl.when((step >= 2) & (step < LAYERS + 2))
        def _():
            add_middle(LAYERS + 1 - step)

        @pl.when((step >= 3) & (step < LAYERS + 3))
        def _():
            add_first(LAYERS + 2 - step)

        @pl.when(step >= 4)
        def _():
            add_second(LAYERS + 3 - step)

    def backward(step, carry):
        layer = LAYERS - 1 - step
        slot = lax.rem(step + 1, 2)
        now = lax.rem(step, 2)
        finish(exchange(slot, 16 + TOK))
        total = mine[...]
        for i in range(ZN - 1):
            total = total + rcv[slot, i, 16 : 16 + TOK].astype(F32)
        pre = pre_s[layer]
        scale = scale_s[layer]
        sigma = 1.0 / (1.0 + jnp.exp(-pre))
        grad_pre = (total * sigma * (1.0 + pre * (1.0 - sigma))).astype(BF16)
        grad_f = grad_pre.astype(F32)
        inner = jnp.sum(grad_f * pre, axis=1, keepdims=True) * (1.0 / FEAT)
        scaled = (grad_f * wide(scale, RANK)).astype(BF16)

        @pl.when(layer > 0)
        def _():
            on_x = wide(scale * scale * inner, TILE)
            on_q = wide(scale, TILE)
            product = jnp.zeros((TOK, RANK), F32)
            for t in range(CH // TILE):
                q = dot_nt(grad_pre, wd[layer, cols(t), :])
                tile = (
                    gx[now, :, cols(t)].astype(F32) + on_q * q - on_x * xs[layer, :, cols(t)].astype(F32)
                ).astype(BF16)
                gx[1 - now, :, cols(t)] = tile
                product += dot_nt(tile, wu[layer - 1, :, cols(t)])
            mine[...] = product
            snd[1 - slot, 16 : 16 + TOK] = product.astype(BF16)
            begin_exchange(1 - slot, 16 + TOK)

        act = act_s[layer]
        turn = lax.rem(layer, 2)
        for t in range(CH // TILE):
            gbuf[turn, t, 0:RANK] = dot_tn(scaled, xs[layer, :, cols(t)]).astype(BF16)
            gbuf[turn, t, RANK : 2 * RANK] = dot_tn(act, gx[now, :, cols(t)]).astype(BF16)
        for half in (0, 1):
            core_copy(layer, half).start()
        sums(step)
        return carry

    lax.fori_loop(0, LAYERS, backward, 0)

    def rest_of_sums(step, carry):
        sums(step)
        return carry

    lax.fori_loop(LAYERS, LAYERS + 4, rest_of_sums, 0)

    def finish_last(layer, carry):
        @pl.when(layer != pipe)
        def _():
            for copy in last_copies(layer):
                copy.wait_send()
            for which in (0, 1):
                remote(
                    d3s.at[layer], res.at[which, layer],
                    g3_ssem.at[layer, which], g3_rsem.at[which, layer], (dp, layer),
                ).wait_recv()
        return carry

    lax.fori_loop(0, LAYERS, finish_last, 0)
    down = jnp.concatenate([res[0, part].astype(F32) for part in range(LAYERS)], axis=0)
    down_ref[...] = jnp.transpose(down).astype(BF16)
    for part in range(LAYERS):
        up_ref[part * 32 : part * 32 + 32] = res[1, part]


def shards(inputs, targets, adapter_down, adapter_up, value_weight, returns):
    any_spec = pl.BlockSpec(memory_space=pl.ANY)
    vmem = pl.BlockSpec(memory_space=pltpu.VMEM)
    dma = pltpu.SemaphoreType.DMA
    down, up = pl.pallas_call(
        kernel,
        out_shape=(
            jax.ShapeDtypeStruct((TILE, RANK), BF16),
            jax.ShapeDtypeStruct((RANK, TILE), BF16),
        ),
        in_specs=[any_spec, any_spec, any_spec, any_spec, any_spec, vmem],
        out_specs=(vmem, vmem),
        scratch_shapes=[
            pltpu.VMEM((8, CH), F32),
            pltpu.VMEM((8, 128), F32),
            pltpu.VMEM((LAYERS + 1, TOK, CH), BF16),
            pltpu.VMEM((LAYERS, CH, RANK), BF16),
            pltpu.VMEM((LAYERS, RANK, CH), BF16),
            pltpu.VMEM((2, 16 + TOK, RANK), BF16),
            pltpu.VMEM((2, ZN - 1, 16 + TOK, RANK), BF16),
            pltpu.VMEM((TOK, RANK), F32),
            pltpu.VMEM((2, TOK, CH), BF16),
            pltpu.VMEM((LAYERS, TOK, RANK), F32),
            pltpu.VMEM((LAYERS, TOK, RANK), BF16),
            pltpu.VMEM((LAYERS, TOK, 128), F32),
            pltpu.VMEM((2, 4, 2 * RANK, TILE), BF16),
            pltpu.VMEM((LAYERS, 2, 2 * RANK, TILE), BF16),
            pltpu.VMEM((4, 4, 4, 32, TILE), BF16),
            pltpu.VMEM((4, 4, 4, 32, TILE), BF16),
            pltpu.VMEM((2, LAYERS, 2, 2, 32, TILE), BF16),
            pltpu.VMEM((LAYERS, 2, 4, 32, TILE), BF16),
            pltpu.VMEM((LAYERS, 2, 4, 32, TILE), BF16),
            pltpu.VMEM((2, 4, 32, TILE), BF16),
            pltpu.VMEM((2, 4, 32, TILE), BF16),
            pltpu.VMEM((LAYERS, 3, 32, TILE), BF16),
            pltpu.VMEM((LAYERS, 3, 32, TILE), BF16),
            pltpu.VMEM((LAYERS, 32, TILE), BF16),
            pltpu.VMEM((LAYERS, 32, TILE), BF16),
            pltpu.VMEM((2, LAYERS, 32, TILE), BF16),
            dma((ZN - 1,)),
            dma((ZN - 1,)),
            dma,
            dma((2,)),
            dma((2, ZN - 1)),
            dma((2, ZN - 1)),
            dma((2, 3)),
            dma((2, LAYERS)),
            dma((2, 2)),
            dma((2, 2)),
            dma((5,)),
            dma((2, LAYERS, 2)),
            dma((2, LAYERS, 2)),
            dma((2, LAYERS)),
            dma((2, LAYERS)),
            dma((2, 2)),
            dma((LAYERS, 2)),
            dma((4, 2, 2)),
            dma((LAYERS, 2, 2)),
            dma((4, 2, 2)),
            dma((LAYERS, 2, 2)),
            dma((2, 2, 3)),
            dma((LAYERS, 2, 3)),
            dma((LAYERS, 2)),
            dma((2, LAYERS)),
        ],
        compiler_params=pltpu.CompilerParams(
            collective_id=0, has_side_effects=True, vmem_limit_bytes=60 * 1024 * 1024
        ),
        name="relay",
    )(inputs, adapter_down, adapter_up, value_weight, returns, targets)
    return (down.astype(F32)[None], up.astype(F32)[None])


def solution(mesh):
    return jax.shard_map(
        shards,
        mesh=mesh,
        in_specs=(
            P(None, "dp", None),
            P(None, "dp"),
            P("pipe", None, None),
            P("pipe", None, None),
            P(),
            P(),
        ),
        out_specs=(P("pipe", "dp", None), P("pipe", None, "dp")),
        check_vma=False,
    )
```
